256 devices in a mesh: gz: 8 (over y, z_lo), row: 4 (over z_hi), col: 8 (over x, core).
Axes of the slice: x: 4, y: 4, z: 8 (z_hi: 4, z_lo: 2; z = z_hi * 2 + z_lo), core: 2. Of those that a mesh axis runs over, the one named last changes fastest.
Arguments:
- lower_sub: bfloat16 [8, 2048, 8192], P('gz', 'row'), may hold values from -0.0625 to 0.0625
- upper_sub: bfloat16 [8, 8192, 2048], P('gz', None, 'col'), may hold values from -6 to 6
- block_mask: int32 [8, 16, 16], P('gz', 'row', 'col'), may hold values 0 or 1
- front_base: float32 [2048, 2048], P(('row', 'gz'), 'col'), may hold values from -6 to 6
- pivot_inverse: float32 [2, 256, 256], replicated, may hold values from -0.01 to 0.01
- pivot_order: int32 [2, 256], replicated, may hold values from 0 to 255, each once within a row
Outputs:
- factored: float32 [2048, 2048], P(('row', 'gz'), 'col')
The draws below stay inside these ranges and needn't reach their ends.
Inputs may be any that keep to these rules, and one draw needn't show every extreme that they name: Each row of pivot_order is a permutation of 0 .. 255.
All inputs are finite; a program needn't handle non-finite values. No bound on the sum of `block_mask` on one device may be relied on, other than what follows from the above.
Results may differ from the reference program's by a relative error of at most 0.0003.
Values sent between devices are 32-bit elements; how exact they have to be, the bound alone decides.
A program may use at most 64 MiB of HBM per device.

```python
import jax
import jax.numpy as jnp
from jax import lax

M = 2048
W = 8192
BS = 256
PANELS = 2
MBLK = 128
N_GZ = 8


def with_ends(entries, key, smallest, largest):
    extent = entries.shape
    spot = [jax.random.randint(jax.random.fold_in(key, axis), (), 0, extent[axis]) for axis in range(len(extent))]
    entries = entries.at[tuple(spot)].set(smallest)
    longest = extent.index(max(extent))
    spot[longest] = (spot[longest] + 1) % extent[longest]
    return entries.at[tuple(spot)].set(largest)


def shard_levels(stream_key, shape, cuts, smallest, largest):
    loudness, own = 1.0, jax.random.fold_in(stream_key, 6)
    for dim, blocks in cuts:
        draws = jnp.exp(jax.random.uniform(jax.random.fold_in(own, dim), (blocks,), jnp.float32, smallest / len(cuts), largest / len(cuts)))
        loudness = loudness * jnp.repeat(draws, shape[dim] // blocks).reshape([-1 if axis == dim else 1 for axis in range(len(shape))])
    return loudness


def bell_draw(stream_key, extent, spread, bound, shards=(), held_as=jnp.bfloat16):
    gain = shard_levels(stream_key, extent, shards, -0.22, 0.18) if shards else 1.0
    values = jax.random.normal(stream_key, extent, jnp.float32) * spread * gain
    return jnp.minimum(jnp.maximum(values, -bound), bound).astype(held_as)


def setup_inputs(seed: int = 0) -> dict:
    splits = jax.random.split(jax.random.key(seed), 7)
    lower_sub = bell_draw(splits[0], (N_GZ, M, W), W ** -0.5, 0.0625, ((0, 8), (1, 4)))
    upper_sub = bell_draw(splits[1], (N_GZ, W, M), 1.0, 6.0, ((0, 8), (2, 8)))
    block_mask = with_ends((jax.random.randint(splits[2], (N_GZ, M // MBLK, M // MBLK), 0, 4) < 3).astype(jnp.int32), jax.random.fold_in(splits[2], 1), 0, 1)
    front_base = bell_draw(splits[3], (M, M), 1.0, 6.0, ((0, 32), (1, 8)), jnp.float32)
    pivot_inverse = bell_draw(splits[4], (PANELS, BS, BS), 0.0015, 0.01, (), jnp.float32)
    pivot_order = jax.vmap(lambda own: jax.random.permutation(own, BS))(jax.random.split(splits[5], PANELS)).reshape((PANELS, BS)).astype(jnp.int32)
    return dict(lower_sub=lower_sub, upper_sub=upper_sub, block_mask=block_mask, front_base=front_base, pivot_inverse=pivot_inverse, pivot_order=pivot_order)


def expand(tiles, span):
    return jnp.repeat(jnp.repeat(tiles.astype(jnp.float32), span, axis=0), span, axis=1)


def reference(lower_sub, upper_sub, block_mask, front_base, pivot_inverse, pivot_order):
    highest = lax.Precision.HIGHEST

    def add_layer(total, items):
        left_factor, right_factor, tiles = items
        product = jnp.dot(left_factor.astype(jnp.float32), right_factor.astype(jnp.float32), precision=highest)
        return total + product * expand(tiles, MBLK), None

    summed, unused = lax.scan(add_layer, jnp.zeros(front_base.shape, jnp.float32), (lower_sub, upper_sub, block_mask))
    front = front_base + summed
    for panel in range(PANELS):
        start_row = panel * BS
        after_row = start_row + BS
        permuted = front[start_row:after_row][pivot_order[panel]]
        front = front.at[start_row:after_row].set(permuted)
        lower = jnp.dot(front[after_row:, start_row:after_row], pivot_inverse[panel], precision=highest)
        front = front.at[after_row:, start_row:after_row].set(lower)
        front = front.at[after_row:, after_row:].add(-jnp.dot(lower, permuted[:, after_row:], precision=highest))
    return front
```

```python
import functools

import jax
import jax.numpy as jnp
from jax import lax
from jax.experimental import pallas as pl
from jax.experimental.pallas import tpu as pltpu
from jax.sharding import PartitionSpec as P

F32 = jnp.float32
BF16 = jnp.bfloat16
MESH = pl.DeviceIdType.MESH


def split(x):
    hi = x.astype(BF16)
    return hi, (x - hi.astype(F32)).astype(BF16)


def dot(a, b):
    return jnp.dot(a, b, preferred_element_type=F32)


def dot3(x, w_hi, w_lo):
    hi, lo = split(x)
    n = x.shape[0]
    both = dot(jnp.concatenate([hi, lo], axis=0), w_hi)
    return both[:n] + (both[n:] + dot(hi, w_lo))


def kernel(
    ng, nr, nc, steps,
    a_hbm, b_hbm, mask_ref, base_ref, inv_ref, order_v, order_s,
    out_ref,
    a_v, b_v, part, land, own, f0, f1, x0, x1, m_hi, m_lo,
    a_sem, b_sem, rs_send, rs_recv,
    z_send, z_recv, ag_send, ag_recv, x_send, x_recv,
):
    g, r, c = lax.axis_index("gz"), lax.axis_index("row"), lax.axis_index("col")
    bs = inv_ref.shape[1]
    rows = own.shape[0]
    ch = rows // 2
    depth = a_v.shape[3]
    mb = bs // (mask_ref.shape[1] // 2)
    first = r == 0

    def a_copy(h, k):
        return pltpu.make_async_copy(
            a_hbm.at[0, pl.ds(h * bs, bs), pl.ds(k * depth, depth)], a_v.at[h, k], a_sem.at[h, k]
        )

    def b_copy(k):
        return pltpu.make_async_copy(b_hbm.at[0, pl.ds(k * depth, depth), :], b_v.at[k], b_sem.at[k])

    for k in range(steps):
        a_copy(0, k).start()
        b_copy(k).start()
    for k in range(steps):
        a_copy(1, k).start()

    barrier = pltpu.get_barrier_semaphore()

    def greet(axis, me, n):
        @pl.loop(1, n)
        def _(d):
            pl.semaphore_signal(barrier, inc=1, device_id={axis: lax.rem(me + d, n)}, device_id_type=MESH)

    greet("gz", g, ng)
    greet("row", r, nr)
    greet("col", c, nc)

    for p in range(2):
        placer = (lax.broadcasted_iota(jnp.int32, (bs, bs), 0) == order_v[p : p + 1, :]).astype(BF16)
        for plain, ref in zip(split(inv_ref[p]), (m_hi, m_lo)):
            moved = lax.dot_general(plain, placer, (((1,), (1,)), ((), ())), preferred_element_type=F32)
            ref[p] = jnp.where(c == p, plain.astype(F32), moved).astype(BF16)

    def rs_copy(p, i):
        q = p * ng + i
        dest = jnp.where(first, i, q // 2)
        h = jnp.where(first, p, q % 2)
        return dest, pltpu.make_async_remote_copy(
            src_ref=part.at[pl.ds(pl.multiple_of(p * bs + i * ch, ch), ch), :],
            dst_ref=land.at[h, g],
            send_sem=rs_send.at[p, i],
            recv_sem=rs_recv.at[h, g],
            device_id={"gz": dest},
            device_id_type=MESH,
        )

    for p in range(2):
        top = p * bs
        for k in range(steps):
            if p == 0:
                b_copy(k).wait()
            a_copy(p, k).wait()
            term = dot(a_v[p, k], b_v[k])
            if k == 0:
                part[top : top + bs, :] = term
            else:
                part[top : top + bs, :] += term
        for i in range(bs // mb):
            for j in range(bs // mb):
                at = (slice(top + i * mb, top + (i + 1) * mb), slice(j * mb, (j + 1) * mb))
                part[at] = part[at] * mask_ref[0, p * (bs // mb) + i, j].astype(F32)

        @pl.when(g // (ng // 2) == p)
        def _():
            mine = pl.ds(pl.multiple_of(g * rows, rows), rows)
            part[mine, :] = part[mine, :] + base_ref[...]

        if p == 0:
            pl.semaphore_wait(barrier, ng + nr + nc - 3)

        @pl.loop(0, ng)
        def _(d):
            i = lax.rem(d + g, ng)
            dest, copy = rs_copy(p, i)

            @pl.when(dest != g)
            def _():
                copy.start()

    def gather_copy(buf, n, d):
        return pltpu.make_async_remote_copy(
            src_ref=buf.at[g],
            dst_ref=buf.at[g],
            send_sem=ag_send.at[n, d],
            recv_sem=ag_recv.at[n, g],
            device_id={"gz": lax.rem(g + d, ng)},
            device_id_type=MESH,
        )

    def down_copy(buf, n, d):
        return pltpu.make_async_remote_copy(
            src_ref=buf.at[g],
            dst_ref=buf.at[g],
            send_sem=z_send.at[n, d],
            recv_sem=z_recv.at[n],
            device_id={"row": d},
            device_id_type=MESH,
        )

    def share(buf, n):
        @pl.when(first & (c > n))
        def _():
            @pl.loop(1, nr)
            def _(d):
                down_copy(buf, n, d).start()

        @pl.when(jnp.logical_not(first) & (c > n))
        def _():
            down_copy(buf, n, 1).wait_recv()

        @pl.when(first | (c > n))
        def _():
            @pl.loop(1, ng)
            def _(d):
                gather_copy(buf, n, d).start()

    def shared(buf, n):
        @pl.loop(1, ng)
        def _(d):
            s = lax.rem(g + d, ng)
            pltpu.make_async_remote_copy(
                src_ref=buf.at[s],
                dst_ref=buf.at[s],
                send_sem=ag_send.at[n, d],
                recv_sem=ag_recv.at[n, s],
                device_id={"gz": s},
                device_id_type=MESH,
            ).wait_recv()

    def column_copy(src, dst, n, d):
        return pltpu.make_async_remote_copy(
            src_ref=src,
            dst_ref=dst,
            send_sem=x_send.at[n, d],
            recv_sem=x_recv.at[n],
            device_id={"col": d},
            device_id_type=MESH,
        )

    for h in range(2):
        start = jnp.where(first, h * bs + g * ch, g * rows + h * ch)
        total = part[pl.ds(pl.multiple_of(start, ch), ch), :]

        def add(d, total):
            s = lax.rem(g + d, ng)
            pltpu.make_async_remote_copy(
                src_ref=land.at[h, s],
                dst_ref=land.at[h, s],
                send_sem=rs_send.at[h, s],
                recv_sem=rs_recv.at[h, s],
                device_id={"gz": s},
                device_id_type=MESH,
            ).wait_recv()
            return total + land[h, s]

        total = lax.fori_loop(1, ng, add, total)
        own[h * ch : (h + 1) * ch, :] = total
        if h == 0:

            @pl.when(first)
            def _():
                f0[g] = own[:ch, :]
                share(f0, 0)

    @pl.when(c == 0)
    def _():
        x0[...] = own[...]

        @pl.loop(1, nc)
        def _(d):
            column_copy(x0, x0, 0, d).start()

    @pl.when(jnp.logical_not(first))
    def _():
        share(f0, 0)

    @pl.when(c > 0)
    def _():
        column_copy(x0, x0, 0, 1).wait_recv()

    left = dot3(x0[...], m_hi[0], m_lo[0])

    @pl.when(first | (c > 0))
    def _():
        shared(f0, 0)

    @pl.when(c == 0)
    def _():
        own[...] = left

    @pl.when(c > 0)
    def _():
        hi, lo = split(f0[...].reshape(bs, -1))
        own[...] = own[...] - dot3(left, hi, lo)

    @pl.when(first)
    def _():
        f1[g] = own[ch:, :]
        share(f1, 1)

    @pl.when(jnp.logical_not(first) & (c == 1))
    def _():
        @pl.loop(2, nc)
        def _(d):
            column_copy(own, x1, 1, d).start()

        out_ref[...] = dot3(own[...], m_hi[1], m_lo[1])

    @pl.when(jnp.logical_not(first) & (c == 0))
    def _():
        out_ref[...] = own[...]

    @pl.when(jnp.logical_not(first) & (c > 1))
    def _():
        share(f1, 1)
        column_copy(own, x1, 1, 1).wait_recv()
        lower = dot3(x1[...], m_hi[1], m_lo[1])
        shared(f1, 1)
        hi, lo = split(f1[...].reshape(bs, -1))
        out_ref[...] = own[...] - dot3(lower, hi, lo)

    @pl.when(first)
    def _():
        shared(f1, 1)

        def place(buf, p):
            @pl.loop(0, rows)
            def _(i):
                src = order_s[p, g % (ng // 2) * rows + i]
                out_ref[pl.ds(i, 1), :] = buf[src // ch, pl.ds(src % ch, 1), :]

        @pl.when(g < ng // 2)
        def _():
            place(f0, 0)

        @pl.when(g >= ng // 2)
        def _():
            place(f1, 1)

    for p in range(2):

        @pl.loop(0, ng)
        def _(i):
            dest, copy = rs_copy(p, i)

            @pl.when(dest != g)
            def _():
                copy.wait_send()

    for n, buf in enumerate((f0, f1)):

        @pl.when(first & (c > n))
        def _():
            @pl.loop(1, nr)
            def _(d):
                down_copy(buf, n, d).wait_send()

        @pl.when(first | (c > n))
        def _():
            @pl.loop(1, ng)
            def _(d):
                gather_copy(buf, n, d).wait_send()

    @pl.when(c == 0)
    def _():
        @pl.loop(1, nc)
        def _(d):
            column_copy(x0, x0, 0, d).wait_send()

    @pl.when(jnp.logical_not(first) & (c == 1))
    def _():
        @pl.loop(2, nc)
        def _(d):
            column_copy(own, x1, 1, d).wait_send()


def on_device(ng, nr, nc, lower_sub, upper_sub, block_mask, front_base, pivot_inverse, pivot_order):
    slab, width = lower_sub.shape[1:]
    rows, cols = front_base.shape
    bs = pivot_inverse.shape[1]
    assert slab == 2 * bs and cols == bs and rows * ng == slab and pivot_inverse.shape[0] == 2
    ch = rows // 2
    steps = 8
    depth = width // steps
    vmem = pl.BlockSpec(memory_space=pltpu.VMEM)
    smem = pl.BlockSpec(memory_space=pltpu.SMEM)
    anywhere = pl.BlockSpec(memory_space=pl.ANY)
    dma = pltpu.SemaphoreType.DMA
    return pl.pallas_call(
        functools.partial(kernel, ng, nr, nc, steps),
        out_shape=jax.ShapeDtypeStruct((rows, cols), F32),
        in_specs=[anywhere, anywhere, smem, vmem, vmem, vmem, smem],
        out_specs=vmem,
        scratch_shapes=[
            pltpu.VMEM((2, steps, bs, depth), BF16),
            pltpu.VMEM((steps, depth, cols), BF16),
            pltpu.VMEM((slab, cols), F32),
            pltpu.VMEM((2, ng, ch, cols), F32),
            pltpu.VMEM((rows, cols), F32),
            pltpu.VMEM((ng, ch, cols), F32),
            pltpu.VMEM((ng, ch, cols), F32),
            pltpu.VMEM((rows, bs), F32),
            pltpu.VMEM((rows, bs), F32),
            pltpu.VMEM((2, bs, bs), BF16),
            pltpu.VMEM((2, bs, bs), BF16),
            dma((2, steps)),
            dma((steps,)),
            dma((2, ng)),
            dma((2, ng)),
            dma((2, nr)),
            dma((2,)),
            dma((2, ng)),
            dma((2, ng)),
            dma((2, nc)),
            dma((2,)),
        ],
        compiler_params=pltpu.CompilerParams(
            collective_id=0, has_side_effects=True, vmem_limit_bytes=48 * 1024 * 1024
        ),
    )(lower_sub, upper_sub, block_mask, front_base, pivot_inverse, pivot_order, pivot_order)


def solution(mesh):
    placed = (
        P("gz", "row", None),
        P("gz", None, "col"),
        P("gz", "row", "col"),
        P(("row", "gz"), "col"),
        P(),
        P(),
    )
    shape = mesh.shape
    return jax.shard_map(
        functools.partial(on_device, shape["gz"], shape["row"], shape["col"]),
        mesh=mesh,
        in_specs=placed,
        out_specs=P(("row", "gz"), "col"),
        check_vma=False,
    )
```

```python
import functools

import jax
import jax.numpy as jnp
from jax import lax
from jax.experimental import pallas as pl
from jax.experimental.pallas import tpu as pltpu
from jax.sharding import PartitionSpec as P

F32 = jnp.float32
BF16 = jnp.bfloat16
VMEM = 63 * 1024 * 1024
MESH = pl.DeviceIdType.MESH


def split(x):
    hi = x.astype(BF16)
    return hi, (x - hi.astype(F32)).astype(BF16)


def dot(a, b):
    return jnp.dot(a, b, preferred_element_type=F32)


def dot3(x, w_hi, w_lo):
    hi, lo = x
    n = hi.shape[0]
    both = dot(jnp.concatenate([hi, lo], axis=0), w_hi)
    return both[:n] + (both[n:] + dot(hi, w_lo))


def kernel(
    ng, nr, nc, steps,
    a_hbm, b_hbm, mask_hbm, base_hbm, inv_hbm, order_hbm,
    out_ref,
    a_v, b_v, mask_ref, base_ref, inv_ref, order_v, order_s,
    part, land, own, raw, f0, f1, x0, x1, m_hi, m_lo,
    a_sem, b_sem, in_sem, rs_send, rs_recv,
    z_send, z_recv, ag_send, ag_recv, x_send, x_recv, s_send, s_recv,
):
    g, r, c = lax.axis_index("gz"), lax.axis_index("row"), lax.axis_index("col")
    bs = inv_ref.shape[1]
    rows = own.shape[0]
    ch = rows // 2
    depth = a_v.shape[1] // steps
    mb = bs // mask_ref.shape[1]
    first = r == 0
    core = lax.rem(c, 2)
    others = jnp.logical_not(first)
    swap = jnp.where(first & (c == 0), 1, 0)
    halves = [slice(j * bs // 2, (j + 1) * bs // 2) for j in range(2)]

    def a_copy(h, k):
        return pltpu.make_async_copy(
            a_hbm.at[0, pl.ds(pl.multiple_of(lax.rem(h + swap, 2) * bs, bs), bs), pl.ds(k * depth, depth)],
            a_v.at[pl.ds(h * bs, bs), pl.ds(k * depth, depth)],
            a_sem.at[h, k],
        )

    def b_copy(k):
        return pltpu.make_async_copy(b_hbm.at[0, pl.ds(k * depth, depth), :], b_v.at[pl.ds(k * depth, depth), :], b_sem.at[k])

    def small(n, src, dst):
        copy = pltpu.make_async_copy(src, dst, in_sem.at[n])
        copy.start()
        return copy

    early = [small(0, mask_hbm, mask_ref), small(1, base_hbm, base_ref)]
    for k in range(steps):
        a_copy(0, k).start()
        b_copy(k).start()
    for k in range(steps):
        a_copy(1, k).start()
    late = [small(2, order_hbm, order_v), small(3, inv_hbm, inv_ref), small(4, order_hbm, order_s)]

    barrier = pltpu.get_barrier_semaphore()

    def greet(axis, me, n):
        @pl.loop(1, n)
        def _(d):
            pl.semaphore_signal(barrier, inc=1, device_id={axis: lax.rem(me + d, n)}, device_id_type=MESH)

    greet("gz", g, ng)
    greet("row", r, nr)
    greet("col", c, nc)

    def rs_copy(p, i):
        half = lax.rem(p + swap, 2)
        q = half * ng + i
        dest = jnp.where(first, i, q // 2)
        h = jnp.where(first, half, lax.rem(q, 2))
        return dest, pltpu.make_async_remote_copy(
            src_ref=part.at[pl.ds(pl.multiple_of(p * bs + i * ch, ch), ch), :],
            dst_ref=land.at[h, g],
            send_sem=rs_send.at[p, i],
            recv_sem=rs_recv.at[h, g],
            device_id={"gz": dest},
            device_id_type=MESH,
        )

    for p in range(2):
        top = p * bs
        half = lax.rem(p + swap, 2)
        at_once = 1 + p
        for k in range(0, steps, at_once):
            for n in range(k, k + at_once):
                if p == 0:
                    b_copy(n).wait()
                a_copy(p, n).wait()
            along = slice(k * depth, (k + at_once) * depth)
            for low in range(top, top + bs, bs // 2):
                term = dot(a_v[low : low + bs // 2, along], b_v[along, :])
                if k == 0:
                    part[low : low + bs // 2, :] = term
                else:
                    part[low : low + bs // 2, :] += term
        if p == 0:
            for copy in early:
                copy.wait()
        for i in range(bs // mb):
            for j in range(bs // mb):
                at = (slice(top + i * mb, top + (i + 1) * mb), slice(j * mb, (j + 1) * mb))
                part[at] = part[at] * mask_ref[0, j, half * (bs // mb) + i].astype(F32)

        @pl.when(g // (ng // 2) == half)
        def _():
            mine = pl.ds(pl.multiple_of(top + lax.rem(g, ng // 2) * rows, rows), rows)
            part[mine, :] = part[mine, :] + base_ref[...]

        if p == 0:
            pl.semaphore_wait(barrier, ng + nr + nc - 3)

        @pl.loop(0, ng)
        def _(d):
            i = lax.rem(d + g, ng)
            dest, copy = rs_copy(p, i)

            @pl.when(dest != g)
            def _():
                copy.start()

    def finish():
        for wait in pending:
            wait()

    def rs_wait():
        for p in range(2):

            @pl.loop(0, ng)
            def _(i):
                dest, copy = rs_copy(p, i)

                @pl.when(dest != g)
                def _():
                    copy.wait_send()

    pending = [rs_wait]

    def gather_copy(buf, n, j, s, d):
        return pltpu.make_async_remote_copy(
            src_ref=buf.at[j, s],
            dst_ref=buf.at[j, s],
            send_sem=ag_send.at[n, j, d],
            recv_sem=ag_recv.at[n, j, s],
            device_id={"gz": lax.rem(g + d, ng)},
            device_id_type=MESH,
        )

    def down(m, act):
        ref = (f0.at[0, g], f0.at[1, g], raw, x0.at[pl.ds(rows, ch), :])[m]

        @pl.loop(1, nr)
        def _(d):
            act(
                pltpu.make_async_remote_copy(
                    src_ref=ref,
                    dst_ref=ref,
                    send_sem=z_send.at[m, d],
                    recv_sem=z_recv.at[m],
                    device_id={"row": d},
                    device_id_type=MESH,
                )
            )

    def downs(m, act):
        pl.when(first & (c == 0 if m == 3 else c > m // 2))(lambda: down(m, act))

    def arrived(m):
        ref = (f0.at[0, g], f0.at[1, g], raw, x0.at[pl.ds(rows, ch), :])[m]
        pltpu.make_async_remote_copy(
            src_ref=ref,
            dst_ref=ref,
            send_sem=z_send.at[m, 1],
            recv_sem=z_recv.at[m],
            device_id={"row": 0},
            device_id_type=MESH,
        ).wait_recv()

    def gather(buf, n, j, act):
        @pl.when(first | (c > n))
        def _():
            @pl.loop(1, ng)
            def _(d):
                reads = jnp.logical_not(first) | (lax.rem(g + d, ng) >= n * (ng // 2))

                @pl.when(reads)
                def _():
                    act(gather_copy(buf, n, j, g, d))

    def begin(copy):
        copy.start()

    def end(copy):
        copy.wait_send()

    def shared(buf, n, j):
        @pl.loop(1, ng)
        def _(d):
            gather_copy(buf, n, j, lax.rem(g + d, ng), d).wait_recv()

    def column_part(m, which=None):
        if m == 2:
            return x1 if which is None else x1.at[which]
        top, size = ((0, rows), (rows, ch))[m]
        if which is None:
            return x0.at[pl.ds(top, size), :]
        return x0.at[pl.ds(pl.multiple_of(top + which * (size // 2), size // 2), size // 2), :]

    def column_copy(m, d, which=None):
        ref = column_part(m, which)
        return pltpu.make_async_remote_copy(
            src_ref=ref,
            dst_ref=ref,
            send_sem=x_send.at[m, d],
            recv_sem=x_recv.at[m],
            device_id={"col": d},
            device_id_type=MESH,
        )

    def sibling_copy(m, which):
        ref = column_part(m, which)
        return pltpu.make_async_remote_copy(
            src_ref=ref,
            dst_ref=ref,
            send_sem=s_send.at[m],
            recv_sem=s_recv.at[m],
            device_id={"col": c + 1 - 2 * core},
            device_id_type=MESH,
        )

    def columns(m, act, only=None):
        @pl.when(c == 0 if m == 1 else others & (c == m // 2))
        def _():
            if m < 2:
                pl.when(first if m == 1 else others)(lambda: act(column_copy(m, 1)))

            @pl.loop(2, nc)
            def _(d):
                if only is None:
                    act(column_copy(m, d, lax.rem(d, 2)))
                else:
                    pl.when(lax.rem(d, 2) == only)(lambda: act(column_copy(m, d, only)))

    def pass_on(m):
        column_copy(m, 1, core).wait_recv()
        sibling_copy(m, core).start()

    def passed_on(m):
        sibling_copy(m, 1 - core).wait_recv()

    for copy in late:
        copy.wait()

    for p in range(2):
        placer = (lax.broadcasted_iota(jnp.int32, (bs, bs), 0) == order_v[p : p + 1, :]).astype(BF16)
        for plain, ref in zip(split(inv_ref[p]), (m_hi, m_lo)):
            moved = lax.dot_general(plain, placer, (((1,), (1,)), ((), ())), preferred_element_type=F32)
            ref[p] = jnp.where(c == p, plain.astype(F32), moved).astype(BF16)

    for n in range(2):
        h = lax.rem(n + swap, 2)
        start = jnp.where(first, n * bs + g * ch, g * rows + n * ch)
        total = part[pl.ds(pl.multiple_of(start, ch), ch), :]

        def add(d, total):
            s = lax.rem(g + d, ng)
            pltpu.make_async_remote_copy(
                src_ref=land.at[h, s],
                dst_ref=land.at[h, s],
                send_sem=rs_send.at[n, s],
                recv_sem=rs_recv.at[h, s],
                device_id={"gz": s},
                device_id_type=MESH,
            ).wait_recv()
            return total + land[h, s]

        total = lax.fori_loop(1, ng, add, total)
        own[pl.ds(pl.multiple_of(h * ch, ch), ch), :] = total

        def panel_0_rows():
            for j, cols in enumerate(halves):
                f0[j, g] = own[:ch, cols]

        def panel_1_rows():
            raw[...] = own[ch:, :]

        if n == 0:

            @pl.when(first & (c == 0))
            def _():
                x0[:rows, :] = jnp.zeros((rows, bs), F32)
                x0[rows:, :] = own[ch:, :]
                columns(1, begin)

            pl.when(first & (c > 0))(panel_0_rows)
            for m in (3, 0, 1):
                downs(m, begin)
        else:
            pl.when(first & (c > 0))(panel_1_rows)
            pl.when(first & (c == 0))(panel_0_rows)
            downs(2, begin)

            @pl.when(first)
            def _():
                for j in range(2):
                    gather(f0, 0, j, begin)

    @pl.when(others & (c == 0))
    def _():
        x0[:rows, :] = own[...]
        columns(0, begin)
        arrived(3)
        columns(1, begin)

    @pl.when(others & (c > 0))
    def _():
        for j in range(2):
            arrived(j)
            gather(f0, 0, j, begin)

    @pl.when(others & (c == 1))
    def _():
        column_copy(0, 1).wait_recv()

    @pl.when(first & (c == 1))
    def _():
        column_copy(1, 1).wait_recv()

    @pl.when(others & (c > 1))
    def _():
        pass_on(0)

    @pl.when(c > 1)
    def _():
        pass_on(1)
        passed_on(1)

    @pl.when(others & (c > 1))
    def _():
        passed_on(0)

    left = dot3(split(x0[...]), m_hi[0], m_lo[0])
    left_parts = split(left)

    @pl.when(others & (c > 1))
    def _():
        arrived(2)

    for j, cols in enumerate(halves):

        @pl.when(first | (c > 0))
        def _():
            shared(f0, 0, j)

        @pl.when(c == 0)
        def _():
            own[:, cols] = left[:rows, cols]
            f1[j, g] = left[rows:, cols]

        @pl.when(c > 0)
        def _():
            update = dot3(left_parts, *split(f0[j].reshape(bs, -1)))
            f1[j, g] = raw[:, cols] - update[rows:]
            own[:, cols] = own[:, cols] - update[:rows]

        gather(f1, 1, j, begin)

        @pl.when(others & (c == 1))
        def _():
            x1[j] = own[:, cols]

        columns(2, begin, j)

    def all_sent():
        for m in range(4):
            downs(m, end)
        for m in range(3):
            columns(m, end)

            @pl.when((others | (m == 1)) & (c > 1))
            def _():
                sibling_copy(m, core).wait_send()

        for n, buf in enumerate((f0, f1)):
            for j in range(2):
                gather(buf, n, j, end)

    pending.append(all_sent)

    @pl.when(others & (c == 1))
    def _():
        out_ref[...] = dot3(split(own[...]), m_hi[1], m_lo[1])

    @pl.when(others & (c == 0))
    def _():
        out_ref[...] = own[...]

    @pl.when(others & (c > 1))
    def _():
        pass_on(2)
        passed_on(2)
        lower = 0.0
        for j, cols in enumerate(halves):
            lower = lower + dot3(split(x1[j]), m_hi[1, cols, :], m_lo[1, cols, :])
        lower_parts = split(lower)
        for j, cols in enumerate(halves):
            shared(f1, 1, j)
            out_ref[:, cols] = own[:, cols] - dot3(lower_parts, *split(f1[j].reshape(bs, -1)))

    @pl.when(first)
    def _():
        def place(buf, p):
            @pl.loop(0, rows)
            def _(i):
                src = order_s[p, g % (ng // 2) * rows + i]
                row = [buf[j, src // ch, pl.ds(src % ch, 1), :] for j in range(2)]
                out_ref[pl.ds(i, 1), :] = jnp.concatenate(row, axis=1)

        @pl.when(g < ng // 2)
        def _():
            place(f0, 0)

        @pl.when(g >= ng // 2)
        def _():
            for j in range(2):
                shared(f1, 1, j)
            place(f1, 1)

    finish()


def on_device(ng, nr, nc, lower_sub, upper_sub, block_mask, front_base, pivot_inverse, pivot_order):
    slab, width = lower_sub.shape[1:]
    rows, cols = front_base.shape
    bs = pivot_inverse.shape[1]
    assert slab == 2 * bs and cols == bs and rows * ng == slab and pivot_inverse.shape[0] == 2
    ch = rows // 2
    steps = 8
    tiles = jnp.swapaxes(block_mask, 1, 2)
    vmem = pl.BlockSpec(memory_space=pltpu.VMEM)
    hbm = pl.BlockSpec(memory_space=pltpu.HBM)
    dma = pltpu.SemaphoreType.DMA
    return pl.pallas_call(
        functools.partial(kernel, ng, nr, nc, steps),
        out_shape=jax.ShapeDtypeStruct((rows, cols), F32),
        in_specs=[hbm] * 6,
        out_specs=vmem,
        scratch_shapes=[
            pltpu.VMEM((slab, width), BF16),
            pltpu.VMEM((width, cols), BF16),
            pltpu.SMEM(tiles.shape, jnp.int32),
            pltpu.VMEM((rows, cols), F32),
            pltpu.VMEM(pivot_inverse.shape, F32),
            pltpu.VMEM(pivot_order.shape, jnp.int32),
            pltpu.SMEM(pivot_order.shape, jnp.int32),
            pltpu.VMEM((slab, cols), F32),
            pltpu.VMEM((2, ng, ch, cols), F32),
            pltpu.VMEM((rows, cols), F32),
            pltpu.VMEM((ch, cols), F32),
            pltpu.VMEM((2, ng, ch, cols // 2), F32),
            pltpu.VMEM((2, ng, ch, cols // 2), F32),
            pltpu.VMEM((rows + ch, bs), F32),
            pltpu.VMEM((2, rows, bs // 2), F32),
            pltpu.VMEM((2, bs, bs), BF16),
            pltpu.VMEM((2, bs, bs), BF16),
            dma((2, steps)),
            dma((steps,)),
            dma((5,)),
            dma((2, ng)),
            dma((2, ng)),
            dma((4, nr)),
            dma((4,)),
            dma((2, 2, ng)),
            dma((2, 2, ng)),
            dma((3, nc)),
            dma((3,)),
            dma((3,)),
            dma((3,)),
        ],
        compiler_params=pltpu.CompilerParams(
            collective_id=0, has_side_effects=True, vmem_limit_bytes=VMEM
        ),
    )(lower_sub, upper_sub, tiles, front_base, pivot_inverse, pivot_order)


def solution(mesh):
    placed = (
        P("gz", "row", None),
        P("gz", None, "col"),
        P("gz", "row", "col"),
        P(("row", "gz"), "col"),
        P(),
        P(),
    )
    shape = mesh.shape
    return jax.shard_map(
        functools.partial(on_device, shape["gz"], shape["row"], shape["col"]),
        mesh=mesh,
        in_specs=placed,
        out_specs=P(("row", "gz"), "col"),
        check_vma=False,
    )
```

```python
import functools

import jax
import jax.numpy as jnp
from jax import lax
from jax.experimental import pallas as pl
from jax.experimental.pallas import tpu as pltpu
from jax.sharding import PartitionSpec as P

F32 = jnp.float32
BF16 = jnp.bfloat16
VMEM = 63 * 1024 * 1024
MESH = pl.DeviceIdType.MESH


def split(x):
    hi = x.astype(BF16)
    return hi, (x - hi.astype(F32)).astype(BF16)


def dot(a, b):
    return jnp.dot(a, b, preferred_element_type=F32)


def dot3(x, w_hi, w_lo):
    hi, lo = x
    n = hi.shape[0]
    both = dot(jnp.concatenate([hi, lo], axis=0), w_hi)
    return both[:n] + (both[n:] + dot(hi, w_lo))


def kernel(
    ng, nr, nc, steps,
    a_hbm, b_hbm, mask_hbm, base_hbm, inv_hbm, order_hbm,
    out_ref,
    a_v, b_v, mask_ref, base_ref, inv_ref, order_v, order_s,
    part, land, own, raw, f0, f1, x0, x1, m_hi, m_lo,
    a_sem, b_sem, in_sem, rs_send, rs_recv,
    z_send, z_recv, ag_send, ag_recv, x_send, x_recv, s_send, s_recv,
):
    g, r, c = lax.axis_index("gz"), lax.axis_index("row"), lax.axis_index("col")
    bs = inv_ref.shape[1]
    rows = own.shape[0]
    ch = rows // 2
    depth = a_v.shape[1] // steps
    mb = bs // mask_ref.shape[1]
    first = r == 0
    core = lax.rem(c, 2)
    others = jnp.logical_not(first)
    swap = jnp.where(first & (c == 0), 1, 0)
    halves = [slice(j * bs // 2, (j + 1) * bs // 2) for j in range(2)]

    def a_copy(h, k):
        return pltpu.make_async_copy(
            a_hbm.at[0, pl.ds(pl.multiple_of(lax.rem(h + swap, 2) * bs, bs), bs), pl.ds(k * depth, depth)],
            a_v.at[pl.ds(h * bs, bs), pl.ds(k * depth, depth)],
            a_sem.at[h, k],
        )

    def b_copy(k):
        return pltpu.make_async_copy(b_hbm.at[0, pl.ds(k * depth, depth), :], b_v.at[pl.ds(k * depth, depth), :], b_sem.at[k])

    def small(n, src, dst):
        copy = pltpu.make_async_copy(src, dst, in_sem.at[n])
        copy.start()
        return copy

    early = [small(0, mask_hbm, mask_ref), small(1, base_hbm, base_ref)]
    for k in range(steps):
        a_copy(0, k).start()
        b_copy(k).start()
    for k in range(steps):
        a_copy(1, k).start()
    late = [small(2, order_hbm, order_v), small(3, inv_hbm, inv_ref), small(4, order_hbm, order_s)]

    barrier = pltpu.get_barrier_semaphore()

    def greet(axis, me, n):
        @pl.loop(1, n)
        def _(d):
            pl.semaphore_signal(barrier, inc=1, device_id={axis: lax.rem(me + d, n)}, device_id_type=MESH)

    greet("gz", g, ng)
    greet("row", r, nr)
    greet("col", c, nc)

    def landed(ref, sem):
        pltpu.make_async_remote_copy(
            src_ref=ref, dst_ref=ref, send_sem=sem, recv_sem=sem, device_id={"gz": g}, device_id_type=MESH
        ).wait_recv()

    def sent(ref, sem):
        pltpu.make_async_remote_copy(
            src_ref=ref, dst_ref=ref, send_sem=sem, recv_sem=sem, device_id={"gz": g}, device_id_type=MESH
        ).wait_send()

    def strips(n):
        return part.at[pl.ds(0, n * ch), :]

    def rs_copy(p, i):
        half = lax.rem(p + swap, 2)
        q = half * ng + i
        dest = jnp.where(first, i, q // 2)
        h = jnp.where(first, half, lax.rem(q, 2))
        return dest, pltpu.make_async_remote_copy(
            src_ref=part.at[pl.ds(pl.multiple_of(p * bs + i * ch, ch), ch), :],
            dst_ref=land.at[h, g],
            send_sem=rs_send,
            recv_sem=rs_recv.at[h],
            device_id={"gz": dest},
            device_id_type=MESH,
        )

    for p in range(2):
        top = p * bs
        half = lax.rem(p + swap, 2)
        at_once = (1, steps // 2)[p]
        for k in range(0, steps, at_once):
            for n in range(k, k + at_once):
                if p == 0:
                    b_copy(n).wait()
                a_copy(p, n).wait()
            along = slice(k * depth, (k + at_once) * depth)
            for low in range(top, top + bs, bs // 2):
                term = dot(a_v[low : low + bs // 2, along], b_v[along, :])
                if k == 0:
                    part[low : low + bs // 2, :] = term
                else:
                    part[low : low + bs // 2, :] += term
        if p == 0:
            for copy in early:
                copy.wait()
        for i in range(bs // mb):
            for j in range(bs // mb):
                at = (slice(top + i * mb, top + (i + 1) * mb), slice(j * mb, (j + 1) * mb))
                part[at] = part[at] * mask_ref[0, j, half * (bs // mb) + i].astype(F32)

        @pl.when(g // (ng // 2) == half)
        def _():
            mine = pl.ds(pl.multiple_of(top + lax.rem(g, ng // 2) * rows, rows), rows)
            part[mine, :] = part[mine, :] + base_ref[...]

        if p == 0:
            pl.semaphore_wait(barrier, ng + nr + nc - 3)

        @pl.loop(0, ng)
        def _(d):
            i = lax.rem(d + g, ng)
            dest, copy = rs_copy(p, i)

            @pl.when(dest != g)
            def _():
                copy.start()

    def gather_copy(buf, n, j, d):
        return pltpu.make_async_remote_copy(
            src_ref=buf.at[j, g],
            dst_ref=buf.at[j, g],
            send_sem=ag_send.at[n, j],
            recv_sem=ag_recv.at[n, j],
            device_id={"gz": lax.rem(g + d, ng)},
            device_id_type=MESH,
        )

    def down_ref(m):
        return (f0.at[0, g], f0.at[1, g], raw.at[0], raw.at[1], x0.at[pl.ds(rows, ch), :])[m]

    def down_copy(m, d):
        return pltpu.make_async_remote_copy(
            src_ref=down_ref(m),
            dst_ref=down_ref(m),
            send_sem=z_send.at[m],
            recv_sem=z_recv.at[m],
            device_id={"row": d},
            device_id_type=MESH,
        )

    def down(m):
        @pl.when(first & (c == 0 if m == 4 else c > m // 2))
        def _():
            @pl.loop(1, nr)
            def _(d):
                down_copy(m, d).start()

    def down_end(m):
        @pl.when(first & (c == 0 if m == 4 else c > m // 2))
        def _():
            sent(strips(nr - 1) if m == 4 else f0.at[0, pl.ds(0, nr - 1)], z_send.at[m])

    def arrived(m):
        down_copy(m, 0).wait_recv()

    def gather(buf, n, j):
        @pl.when(first | (c > n))
        def _():
            @pl.loop(1, ng)
            def _(d):
                reads = others | (lax.rem(g + d, ng) >= n * (ng // 2))

                @pl.when(reads)
                def _():
                    gather_copy(buf, n, j, d).start()

    def gather_end(buf, n, j):
        def ended(count):
            sent(buf.at[j, pl.ds(0, count)], ag_send.at[n, j])

        if n == 0:
            pl.when(first | (c > n))(lambda: ended(ng - 1))
        else:
            pl.when(others & (c > n))(lambda: ended(ng - 1))
            pl.when(first & (g < ng // 2))(lambda: ended(ng // 2))
            if ng > 2:
                pl.when(first & (g >= ng // 2))(lambda: ended(ng // 2 - 1))

    def shared(buf, n, j):
        landed(buf.at[j, pl.ds(0, ng - 1)], ag_recv.at[n, j])

    def column_part(m, which=None):
        if m == 1:
            return x0.at[pl.ds(rows, ch), :]
        if m == 2:
            return x1.at[which]
        if which is None:
            return x0.at[pl.ds(0, rows), :]
        return x0.at[pl.ds(pl.multiple_of(which * ch, ch), ch), :]

    def column_copy(m, d, which=None):
        ref = column_part(m, which)
        return pltpu.make_async_remote_copy(
            src_ref=ref,
            dst_ref=ref,
            send_sem=x_send.at[m],
            recv_sem=x_recv.at[m],
            device_id={"col": d},
            device_id_type=MESH,
        )

    def sibling_copy(m, which):
        ref = column_part(m, which)
        return pltpu.make_async_remote_copy(
            src_ref=ref,
            dst_ref=ref,
            send_sem=s_send.at[m],
            recv_sem=s_recv.at[m],
            device_id={"col": c + 1 - 2 * core},
            device_id_type=MESH,
        )

    def columns(m, only=None):
        @pl.when(c == 0 if m == 1 else others & (c == m // 2))
        def _():
            @pl.loop(1 if m == 1 else 2, nc)
            def _(d):
                if m == 1:
                    pl.when(first | (d > 1))(lambda: column_copy(m, d).start())
                elif only is None:
                    column_copy(m, d, lax.rem(d, 2)).start()
                else:
                    pl.when(lax.rem(d, 2) == only)(lambda: column_copy(m, d, only).start())

    def columns_end(m):
        if m == 1:
            pl.when(first & (c == 0))(lambda: sent(strips(nc - 1), x_send.at[m]))
            pl.when(others & (c == 0))(lambda: sent(strips(nc - 2), x_send.at[m]))
        else:
            count = nc if m == 0 else nc - 2
            pl.when(others & (c == m // 2))(lambda: sent(strips(count), x_send.at[m]))

    def pass_on(m):
        column_copy(m, 1, core).wait_recv()
        sibling_copy(m, core).start()

    def passed_on(m):
        sibling_copy(m, 1 - core).wait_recv()

    for copy in late:
        copy.wait()

    for p in range(2):
        placer = (lax.broadcasted_iota(jnp.int32, (bs, bs), 0) == order_v[p : p + 1, :]).astype(BF16)
        for plain, ref in zip(split(inv_ref[p]), (m_hi, m_lo)):
            moved = lax.dot_general(plain, placer, (((1,), (1,)), ((), ())), preferred_element_type=F32)
            ref[p] = jnp.where(c == p, plain.astype(F32), moved).astype(BF16)

    for n in range(2):
        h = lax.rem(n + swap, 2)
        start = jnp.where(first, n * bs + g * ch, g * rows + n * ch)
        landed(land.at[h, pl.ds(0, ng - 1)], rs_recv.at[h])
        land[h, g] = part[pl.ds(pl.multiple_of(start, ch), ch), :]
        total = land[h, 0]
        for m in range(1, ng):
            total = total + land[h, m]
        own[pl.ds(pl.multiple_of(h * ch, ch), ch), :] = total

        def panel_0_rows():
            for j, cols in enumerate(halves):
                f0[j, g] = own[:ch, cols]

        def panel_1_rows():
            for j, cols in enumerate(halves):
                raw[j] = own[ch:, cols]

        if n == 0:

            @pl.when(first & (c == 0))
            def _():
                x0[rows:, :] = own[ch:, :]
                columns(1)

            pl.when(first & (c > 0))(panel_0_rows)
            for m in (4, 0, 1):
                down(m)
        else:
            pl.when(first & (c > 0))(panel_1_rows)
            pl.when(first & (c == 0))(panel_0_rows)
            down(2)
            down(3)

            @pl.when(first)
            def _():
                for j in range(2):
                    gather(f0, 0, j)

    @pl.when(others & (c == 0))
    def _():
        x0[:rows, :] = own[...]
        column_copy(0, 1).start()
        arrived(4)
        columns(1)
        columns(0)

    @pl.when(others & (c > 0))
    def _():
        for j in range(2):
            arrived(j)
            gather(f0, 0, j)

    @pl.when(first | (c > 1))
    def _():
        @pl.when(c > 0)
        def _():
            column_copy(1, 1).wait_recv()

        lower = dot3(split(x0[rows:, :]), m_hi[0], m_lo[0])
        parts = split(lower)

        for j, cols in enumerate(halves):

            @pl.when(others)
            def _():
                arrived(2 + j)

            shared(f0, 0, j)

            @pl.when(c == 0)
            def _():
                f1[j, g] = lower[:, cols]

            @pl.when(c > 0)
            def _():
                f1[j, g] = raw[j] - dot3(parts, *split(f0[j].reshape(bs, -1)))

            gather(f1, 1, j)

    @pl.when(others)
    def _():
        @pl.when(c == 1)
        def _():
            column_copy(0, 1).wait_recv()

        @pl.when(c > 1)
        def _():
            pass_on(0)
            passed_on(0)

        lower = dot3(split(x0[:rows, :]), m_hi[0], m_lo[0])
        parts = split(lower)

        @pl.when(c == 0)
        def _():
            own[...] = lower

        @pl.when(c > 0)
        def _():
            for j, cols in enumerate(halves):

                @pl.when(c == 1)
                def _():
                    shared(f0, 0, j)

                own[:, cols] = own[:, cols] - dot3(parts, *split(f0[j].reshape(bs, -1)))

                @pl.when(c == 1)
                def _():
                    x1[j] = own[:, cols]
                    columns(2, j)

    sent(strips(2 * (ng - 1)), rs_send)
    for m in range(5):
        down_end(m)
    for m in range(2):
        columns_end(m)
    for j in range(2):
        gather_end(f0, 0, j)
    pl.when(others & (c > 1))(lambda: sibling_copy(0, core).wait_send())

    @pl.when(others & (c == 1))
    def _():
        out_ref[...] = dot3(split(own[...]), m_hi[1], m_lo[1])

    @pl.when(others & (c == 0))
    def _():
        out_ref[...] = own[...]

    @pl.when(others & (c > 1))
    def _():
        pass_on(2)
        passed_on(2)
        lower = 0.0
        for j, cols in enumerate(halves):
            lower = lower + dot3(split(x1[j]), m_hi[1, cols, :], m_lo[1, cols, :])
        lower_parts = split(lower)
        for j, cols in enumerate(halves):
            shared(f1, 1, j)
            out_ref[:, cols] = own[:, cols] - dot3(lower_parts, *split(f1[j].reshape(bs, -1)))

    @pl.when(first)
    def _():
        def place(buf, p):
            @pl.loop(0, rows, unroll=8)
            def _(i):
                src = order_s[p, g % (ng // 2) * rows + i]
                row = [buf[j, src // ch, pl.ds(src % ch, 1), :] for j in range(2)]
                out_ref[pl.ds(i, 1), :] = jnp.concatenate(row, axis=1)

        @pl.when(g < ng // 2)
        def _():
            place(f0, 0)

        @pl.when(g >= ng // 2)
        def _():
            for j in range(2):
                shared(f1, 1, j)
            place(f1, 1)

    columns_end(2)
    for j in range(2):
        gather_end(f1, 1, j)
    pl.when(others & (c > 1))(lambda: sibling_copy(2, core).wait_send())


def on_device(ng, nr, nc, lower_sub, upper_sub, block_mask, front_base, pivot_inverse, pivot_order):
    slab, width = lower_sub.shape[1:]
    rows, cols = front_base.shape
    bs = pivot_inverse.shape[1]
    assert slab == 2 * bs and cols == bs and rows * ng == slab and pivot_inverse.shape[0] == 2
    ch = rows // 2
    steps = 8
    tiles = jnp.swapaxes(block_mask, 1, 2)
    vmem = pl.BlockSpec(memory_space=pltpu.VMEM)
    hbm = pl.BlockSpec(memory_space=pltpu.HBM)
    dma = pltpu.SemaphoreType.DMA
    return pl.pallas_call(
        functools.partial(kernel, ng, nr, nc, steps),
        out_shape=jax.ShapeDtypeStruct((rows, cols), F32),
        in_specs=[hbm] * 6,
        out_specs=vmem,
        scratch_shapes=[
            pltpu.VMEM((slab, width), BF16),
            pltpu.VMEM((width, cols), BF16),
            pltpu.SMEM(tiles.shape, jnp.int32),
            pltpu.VMEM((rows, cols), F32),
            pltpu.VMEM(pivot_inverse.shape, F32),
            pltpu.VMEM(pivot_order.shape, jnp.int32),
            pltpu.SMEM(pivot_order.shape, jnp.int32),
            pltpu.VMEM((slab, cols), F32),
            pltpu.VMEM((2, ng, ch, cols), F32),
            pltpu.VMEM((rows, cols), F32),
            pltpu.VMEM((2, ch, cols // 2), F32),
            pltpu.VMEM((2, ng, ch, cols // 2), F32),
            pltpu.VMEM((2, ng, ch, cols // 2), F32),
            pltpu.VMEM((rows + ch, bs), F32),
            pltpu.VMEM((2, rows, bs // 2), F32),
            pltpu.VMEM((2, bs, bs), BF16),
            pltpu.VMEM((2, bs, bs), BF16),
            dma((2, steps)),
            dma((steps,)),
            dma((5,)),
            dma(()),
            dma((2,)),
            dma((5,)),
            dma((5,)),
            dma((2, 2)),
            dma((2, 2)),
            dma((3,)),
            dma((3,)),
            dma((3,)),
            dma((3,)),
        ],
        compiler_params=pltpu.CompilerParams(
            collective_id=0, has_side_effects=True, vmem_limit_bytes=VMEM
        ),
    )(lower_sub, upper_sub, tiles, front_base, pivot_inverse, pivot_order)


def solution(mesh):
    placed = (
        P("gz", "row", None),
        P("gz", None, "col"),
        P("gz", "row", "col"),
        P(("row", "gz"), "col"),
        P(),
        P(),
    )
    shape = mesh.shape
    return jax.shard_map(
        functools.partial(on_device, shape["gz"], shape["row"], shape["col"]),
        mesh=mesh,
        in_specs=placed,
        out_specs=P(("row", "gz"), "col"),
        check_vma=False,
    )
```

```python
import functools

import jax
import jax.numpy as jnp
from jax import lax
from jax.experimental import pallas as pl
from jax.experimental.pallas import tpu as pltpu
from jax.sharding import PartitionSpec as P

F32 = jnp.float32
BF16 = jnp.bfloat16
VMEM = 48 * 1024 * 1024
MESH = pl.DeviceIdType.MESH


def split(x):
    hi = x.astype(BF16)
    return hi, (x - hi.astype(F32)).astype(BF16)


def dot(a, b):
    return jnp.dot(a, b, preferred_element_type=F32)


def dot3(x, w_hi, w_lo):
    hi, lo = x
    n = hi.shape[0]
    both = dot(jnp.concatenate([hi, lo], axis=0), w_hi)
    return both[:n] + (both[n:] + dot(hi, w_lo))


def kernel(
    ng, nr, nc, steps,
    a_hbm, b_hbm, mask_hbm, base_hbm, inv_hbm, order_hbm,
    out_ref,
    a_v, b_v, mask_ref, base_ref, inv_ref, order_v, order_s,
    part, land, own, raw, f0, f1, x0, x1, m_hi, m_lo,
    a_sem, b_sem, in_sem, rs_send, rs_recv,
    z_send, z_recv, ag_send, ag_recv, x_send, x_recv, s_send, s_recv,
):
    g, r, c = lax.axis_index("gz"), lax.axis_index("row"), lax.axis_index("col")
    bs = inv_ref.shape[1]
    rows = own.shape[0]
    ch = rows // 2
    depth = a_v.shape[1] // steps
    mb = bs // mask_ref.shape[1]
    first = r == 0
    core = lax.rem(c, 2)
    others = jnp.logical_not(first)
    swap = jnp.where(first & (c == 0), 1, 0)
    halves = [slice(j * bs // 2, (j + 1) * bs // 2) for j in range(2)]

    def a_copy(h, k):
        return pltpu.make_async_copy(
            a_hbm.at[0, pl.ds(pl.multiple_of(lax.rem(h + swap, 2) * bs, bs), bs), pl.ds(k * depth, depth)],
            a_v.at[pl.ds(h * bs, bs), pl.ds(k * depth, depth)],
            a_sem.at[h, k],
        )

    def b_copy(k):
        return pltpu.make_async_copy(b_hbm.at[0, pl.ds(k * depth, depth), :], b_v.at[pl.ds(k * depth, depth), :], b_sem.at[k])

    def small(n, src, dst):
        copy = pltpu.make_async_copy(src, dst, in_sem.at[n])
        copy.start()
        return copy

    early = [small(0, mask_hbm, mask_ref), small(1, base_hbm, base_ref)]
    for k in range(steps):
        a_copy(0, k).start()
        b_copy(k).start()
    for k in range(steps):
        a_copy(1, k).start()
    late = [small(2, order_hbm, order_v), small(3, inv_hbm, inv_ref), small(4, order_hbm, order_s)]

    barrier = pltpu.get_barrier_semaphore()

    def greet(axis, me, n):
        @pl.loop(1, n)
        def _(d):
            pl.semaphore_signal(barrier, inc=1, device_id={axis: lax.rem(me + d, n)}, device_id_type=MESH)

    greet("gz", g, ng)
    greet("row", r, nr)
    greet("col", c, nc)

    def landed(ref, sem):
        pltpu.make_async_remote_copy(
            src_ref=ref, dst_ref=ref, send_sem=sem, recv_sem=sem, device_id={"gz": g}, device_id_type=MESH
        ).wait_recv()

    def sent(ref, sem):
        pltpu.make_async_remote_copy(
            src_ref=ref, dst_ref=ref, send_sem=sem, recv_sem=sem, device_id={"gz": g}, device_id_type=MESH
        ).wait_send()

    def strips(n):
        return part.at[pl.ds(0, n * ch), :]

    def rs_copy(p, i):
        half = lax.rem(p + swap, 2)
        q = half * ng + i
        dest = jnp.where(first, i, q // 2)
        h = jnp.where(first, half, lax.rem(q, 2))
        return dest, pltpu.make_async_remote_copy(
            src_ref=part.at[pl.ds(pl.multiple_of(p * bs + i * ch, ch), ch), :],
            dst_ref=land.at[h, g],
            send_sem=rs_send,
            recv_sem=rs_recv.at[h],
            device_id={"gz": dest},
            device_id_type=MESH,
        )

    for p in range(2):
        top = p * bs
        half = lax.rem(p + swap, 2)
        at_once = (1, 2)[p]
        for k in range(0, steps, at_once):
            for n in range(k, k + at_once):
                if p == 0:
                    b_copy(n).wait()
                a_copy(p, n).wait()
            along = slice(k * depth, (k + at_once) * depth)
            for low in range(top, top + bs, bs // 2):
                term = dot(a_v[low : low + bs // 2, along], b_v[along, :])
                if k == 0:
                    part[low : low + bs // 2, :] = term
                else:
                    part[low : low + bs // 2, :] += term
        if p == 0:
            for copy in early:
                copy.wait()
        for i in range(bs // mb):
            for j in range(bs // mb):
                at = (slice(top + i * mb, top + (i + 1) * mb), slice(j * mb, (j + 1) * mb))
                part[at] = part[at] * mask_ref[0, j, half * (bs // mb) + i].astype(F32)

        @pl.when(g // (ng // 2) == half)
        def _():
            mine = pl.ds(pl.multiple_of(top + lax.rem(g, ng // 2) * rows, rows), rows)
            part[mine, :] = part[mine, :] + base_ref[...]

        if p == 0:
            pl.semaphore_wait(barrier, ng + nr + nc - 3)

        @pl.loop(0, ng)
        def _(d):
            i = lax.rem(d + g, ng)
            dest, copy = rs_copy(p, i)

            @pl.when(dest != g)
            def _():
                copy.start()

    def gather_copy(buf, n, j, d):
        return pltpu.make_async_remote_copy(
            src_ref=buf.at[j, g],
            dst_ref=buf.at[j, g],
            send_sem=ag_send.at[n, j],
            recv_sem=ag_recv.at[n, j],
            device_id={"gz": lax.rem(g + d, ng)},
            device_id_type=MESH,
        )

    def down_ref(m):
        return (f0.at[0, g], f0.at[1, g], raw.at[0], raw.at[1], x0.at[pl.ds(rows, ch), :])[m]

    def down_copy(m, d):
        return pltpu.make_async_remote_copy(
            src_ref=down_ref(m),
            dst_ref=down_ref(m),
            send_sem=z_send.at[m],
            recv_sem=z_recv.at[m],
            device_id={"row": d},
            device_id_type=MESH,
        )

    def down(m):
        @pl.when(first & (c == 0 if m == 4 else c > m // 2))
        def _():
            @pl.loop(1, nr)
            def _(d):
                down_copy(m, d).start()

    def down_end(m):
        @pl.when(first & (c == 0 if m == 4 else c > m // 2))
        def _():
            sent(strips(nr - 1) if m == 4 else f0.at[0, pl.ds(0, nr - 1)], z_send.at[m])

    def arrived(m):
        down_copy(m, 0).wait_recv()

    def gather(buf, n, j):
        @pl.when(first | (c > n))
        def _():
            @pl.loop(1, ng)
            def _(d):
                reads = others | (lax.rem(g + d, ng) >= n * (ng // 2))

                @pl.when(reads)
                def _():
                    gather_copy(buf, n, j, d).start()

    def gather_end(buf, n, j):
        def ended(count):
            sent(buf.at[j, pl.ds(0, count)], ag_send.at[n, j])

        if n == 0:
            pl.when(first | (c > n))(lambda: ended(ng - 1))
        else:
            pl.when(others & (c > n))(lambda: ended(ng - 1))
            pl.when(first & (g < ng // 2))(lambda: ended(ng // 2))
            if ng > 2:
                pl.when(first & (g >= ng // 2))(lambda: ended(ng // 2 - 1))

    def shared(buf, n, j):
        landed(buf.at[j, pl.ds(0, ng - 1)], ag_recv.at[n, j])

    def column_part(m, which=None):
        if m == 1:
            return x0.at[pl.ds(rows, ch), :]
        if m == 2:
            return x1.at[which]
        if which is None:
            return x0.at[pl.ds(0, rows), :]
        return x0.at[pl.ds(pl.multiple_of(which * ch, ch), ch), :]

    def column_copy(m, d, which=None):
        ref = column_part(m, which)
        return pltpu.make_async_remote_copy(
            src_ref=ref,
            dst_ref=ref,
            send_sem=x_send.at[m],
            recv_sem=x_recv.at[m],
            device_id={"col": d},
            device_id_type=MESH,
        )

    def sibling_copy(m, which):
        ref = column_part(m, which)
        return pltpu.make_async_remote_copy(
            src_ref=ref,
            dst_ref=ref,
            send_sem=s_send.at[m],
            recv_sem=s_recv.at[m],
            device_id={"col": c + 1 - 2 * core},
            device_id_type=MESH,
        )

    def columns(m, only=None):
        @pl.when(c == 0 if m == 1 else others & (c == m // 2))
        def _():
            @pl.loop(1 if m == 1 else 2, nc)
            def _(d):
                if m == 1:
                    pl.when(first | (d > 1))(lambda: column_copy(m, d).start())
                elif only is None:
                    column_copy(m, d, lax.rem(d, 2)).start()
                else:
                    pl.when(lax.rem(d, 2) == only)(lambda: column_copy(m, d, only).start())

    def columns_end(m):
        if m == 1:
            pl.when(first & (c == 0))(lambda: sent(strips(nc - 1), x_send.at[m]))
            pl.when(others & (c == 0))(lambda: sent(strips(nc - 2), x_send.at[m]))
        else:
            count = nc if m == 0 else nc - 2
            pl.when(others & (c == m // 2))(lambda: sent(strips(count), x_send.at[m]))

    def pass_on(m):
        column_copy(m, 1, core).wait_recv()
        sibling_copy(m, core).start()

    def passed_on(m):
        sibling_copy(m, 1 - core).wait_recv()

    for copy in late:
        copy.wait()

    for p in range(2):
        placer = (lax.broadcasted_iota(jnp.int32, (bs, bs), 0) == order_v[p : p + 1, :]).astype(BF16)
        for plain, ref in zip(split(inv_ref[p]), (m_hi, m_lo)):
            moved = lax.dot_general(plain, placer, (((1,), (1,)), ((), ())), preferred_element_type=F32)
            ref[p] = jnp.where(c == p, plain.astype(F32), moved).astype(BF16)

    for n in range(2):
        h = lax.rem(n + swap, 2)
        start = jnp.where(first, n * bs + g * ch, g * rows + n * ch)
        landed(land.at[h, pl.ds(0, ng - 1)], rs_recv.at[h])
        land[h, g] = part[pl.ds(pl.multiple_of(start, ch), ch), :]
        total = land[h, 0]
        for m in range(1, ng):
            total = total + land[h, m]
        own[pl.ds(pl.multiple_of(h * ch, ch), ch), :] = total

        def panel_0_rows():
            for j, cols in enumerate(halves):
                f0[j, g] = own[:ch, cols]

        def panel_1_rows():
            for j, cols in enumerate(halves):
                raw[j] = own[ch:, cols]

        if n == 0:

            @pl.when(first & (c == 0))
            def _():
                x0[rows:, :] = own[ch:, :]
                columns(1)

            pl.when(first & (c > 0))(panel_0_rows)
            for m in (4, 0, 1):
                down(m)
        else:
            pl.when(first & (c > 0))(panel_1_rows)
            pl.when(first & (c == 0))(panel_0_rows)
            down(2)
            down(3)

            @pl.when(first)
            def _():
                for j in range(2):
                    gather(f0, 0, j)

    @pl.when(others & (c == 0))
    def _():
        x0[:rows, :] = own[...]
        column_copy(0, 1).start()
        arrived(4)
        columns(1)
        columns(0)

    @pl.when(others & (c > 0))
    def _():
        for j in range(2):
            arrived(j)
            gather(f0, 0, j)

    @pl.when(first | (c > 1))
    def _():
        @pl.when(c > 0)
        def _():
            column_copy(1, 1).wait_recv()

        lower = dot3(split(x0[rows:, :]), m_hi[0], m_lo[0])
        parts = split(lower)

        for j, cols in enumerate(halves):

            @pl.when(others)
            def _():
                arrived(2 + j)

            shared(f0, 0, j)

            @pl.when(c == 0)
            def _():
                f1[j, g] = lower[:, cols]

            @pl.when(c > 0)
            def _():
                f1[j, g] = raw[j] - dot3(parts, *split(f0[j].reshape(bs, -1)))

            gather(f1, 1, j)

    @pl.when(others)
    def _():
        @pl.when(c == 1)
        def _():
            column_copy(0, 1).wait_recv()

        @pl.when(c > 1)
        def _():
            pass_on(0)
            passed_on(0)

        lower = dot3(split(x0[:rows, :]), m_hi[0], m_lo[0])
        parts = split(lower)

        @pl.when(c == 0)
        def _():
            own[...] = lower

        @pl.when(c > 0)
        def _():
            for j, cols in enumerate(halves):

                @pl.when(c == 1)
                def _():
                    shared(f0, 0, j)

                own[:, cols] = own[:, cols] - dot3(parts, *split(f0[j].reshape(bs, -1)))

                @pl.when(c == 1)
                def _():
                    x1[j] = own[:, cols]
                    columns(2, j)

    sent(strips(2 * (ng - 1)), rs_send)
    for m in range(5):
        down_end(m)
    for m in range(2):
        columns_end(m)
    for j in range(2):
        gather_end(f0, 0, j)
    pl.when(others & (c > 1))(lambda: sibling_copy(0, core).wait_send())

    @pl.when(others & (c == 1))
    def _():
        out_ref[...] = dot3(split(own[...]), m_hi[1], m_lo[1])

    @pl.when(others & (c == 0))
    def _():
        out_ref[...] = own[...]

    @pl.when(others & (c > 1))
    def _():
        pass_on(2)
        passed_on(2)
        lower = 0.0
        for j, cols in enumerate(halves):
            lower = lower + dot3(split(x1[j]), m_hi[1, cols, :], m_lo[1, cols, :])
        lower_parts = split(lower)
        for j, cols in enumerate(halves):
            shared(f1, 1, j)
            out_ref[:, cols] = own[:, cols] - dot3(lower_parts, *split(f1[j].reshape(bs, -1)))

    @pl.when(first)
    def _():
        def place(buf, p):
            @pl.loop(0, rows, unroll=8)
            def _(i):
                src = order_s[p, g % (ng // 2) * rows + i]
                row = [buf[j, src // ch, pl.ds(src % ch, 1), :] for j in range(2)]
                out_ref[pl.ds(i, 1), :] = jnp.concatenate(row, axis=1)

        @pl.when(g < ng // 2)
        def _():
            place(f0, 0)

        @pl.when(g >= ng // 2)
        def _():
            for j in range(2):
                shared(f1, 1, j)
            place(f1, 1)

    columns_end(2)
    for j in range(2):
        gather_end(f1, 1, j)
    pl.when(others & (c > 1))(lambda: sibling_copy(2, core).wait_send())


def on_device(ng, nr, nc, lower_sub, upper_sub, block_mask, front_base, pivot_inverse, pivot_order):
    slab, width = lower_sub.shape[1:]
    rows, cols = front_base.shape
    bs = pivot_inverse.shape[1]
    assert slab == 2 * bs and cols == bs and rows * ng == slab and pivot_inverse.shape[0] == 2
    ch = rows // 2
    steps = 4
    tiles = jnp.swapaxes(block_mask, 1, 2)
    operands = (lower_sub, upper_sub, tiles, front_base, pivot_inverse, pivot_order)
    vmem = pl.BlockSpec(memory_space=pltpu.VMEM)
    hbm = pl.BlockSpec(memory_space=pltpu.HBM)
    dma = pltpu.SemaphoreType.DMA
    return pl.pallas_call(
        functools.partial(kernel, ng, nr, nc, steps),
        out_shape=jax.ShapeDtypeStruct((rows, cols), F32),
        in_specs=[hbm] * 6,
        out_specs=vmem,
        scratch_shapes=[
            pltpu.VMEM((slab, width), BF16),
            pltpu.VMEM((width, cols), BF16),
            pltpu.SMEM(tiles.shape, jnp.int32),
            pltpu.VMEM((rows, cols), F32),
            pltpu.VMEM(pivot_inverse.shape, F32),
            pltpu.VMEM(pivot_order.shape, jnp.int32),
            pltpu.SMEM(pivot_order.shape, jnp.int32),
            pltpu.VMEM((slab, cols), F32),
            pltpu.VMEM((2, ng, ch, cols), F32),
            pltpu.VMEM((rows, cols), F32),
            pltpu.VMEM((2, ch, cols // 2), F32),
            pltpu.VMEM((2, ng, ch, cols // 2), F32),
            pltpu.VMEM((2, ng, ch, cols // 2), F32),
            pltpu.VMEM((rows + ch, bs), F32),
            pltpu.VMEM((2, rows, bs // 2), F32),
            pltpu.VMEM((2, bs, bs), BF16),
            pltpu.VMEM((2, bs, bs), BF16),
            dma((2, steps)),
            dma((steps,)),
            dma((5,)),
            dma(()),
            dma((2,)),
            dma((5,)),
            dma((5,)),
            dma((2, 2)),
            dma((2, 2)),
            dma((3,)),
            dma((3,)),
            dma((3,)),
            dma((3,)),
        ],
        compiler_params=pltpu.CompilerParams(
            collective_id=0, has_side_effects=True, vmem_limit_bytes=VMEM
        ),
    )(*[pltpu.with_memory_space_constraint(x, pltpu.HBM) for x in operands])


def solution(mesh):
    placed = (
        P("gz", "row", None),
        P("gz", None, "col"),
        P("gz", "row", "col"),
        P(("row", "gz"), "col"),
        P(),
        P(),
    )
    shape = mesh.shape
    return jax.shard_map(
        functools.partial(on_device, shape["gz"], shape["row"], shape["col"]),
        mesh=mesh,
        in_specs=placed,
        out_specs=P(("row", "gz"), "col"),
        check_vma=False,
    )
```

```python
import functools

import jax
import jax.numpy as jnp
from jax import lax
from jax.experimental import pallas as pl
from jax.experimental.pallas import tpu as pltpu
from jax.sharding import PartitionSpec as P

F32 = jnp.float32
BF16 = jnp.bfloat16
VMEM = 48 * 1024 * 1024
MESH = pl.DeviceIdType.MESH


def split(x):
    hi = x.astype(BF16)
    return hi, (x - hi.astype(F32)).astype(BF16)


def dot(a, b):
    return jnp.dot(a, b, preferred_element_type=F32)


def dot3(x, w_hi, w_lo):
    hi, lo = x
    n = hi.shape[0]
    both = dot(jnp.concatenate([hi, lo], axis=0), w_hi)
    return both[:n] + (both[n:] + dot(hi, w_lo))


def kernel(
    ng, nr, nc, steps,
    a_hbm, b_hbm, mask_hbm, base_hbm, inv_hbm, order_hbm,
    out_ref,
    a_v, b_v, mask_ref, base_ref, inv_ref, order_v, order_s,
    part, land, own, raw, f0, f1, x0, x1, m_hi, m_lo,
    a_sem, b_sem, in_sem, rs_send, rs_recv,
    z_send, z_recv, ag_send, ag_recv, x_send, x_recv, s_send, s_recv,
):
    g, r, c = lax.axis_index("gz"), lax.axis_index("row"), lax.axis_index("col")
    bs = inv_ref.shape[1]
    rows = own.shape[0]
    ch = rows // 2
    depth = a_v.shape[1] // steps
    mb = bs // mask_ref.shape[1]
    first = r == 0
    core = lax.rem(c, 2)
    far_first = sorted(range(1, ng), key=lambda d: abs(2 * d - ng))
    others = jnp.logical_not(first)
    swap = jnp.where(first & (c == 0), 1, 0)
    halves = [slice(j * bs // 2, (j + 1) * bs // 2) for j in range(2)]

    def a_copy(h, k):
        return pltpu.make_async_copy(
            a_hbm.at[0, pl.ds(pl.multiple_of(lax.rem(h + swap, 2) * bs, bs), bs), pl.ds(k * depth, depth)],
            a_v.at[pl.ds(h * bs, bs), pl.ds(k * depth, depth)],
            a_sem.at[h, k],
        )

    def b_copy(k):
        return pltpu.make_async_copy(b_hbm.at[0, pl.ds(k * depth, depth), :], b_v.at[pl.ds(k * depth, depth), :], b_sem.at[k])

    def small(n, src, dst):
        copy = pltpu.make_async_copy(src, dst, in_sem.at[n])
        copy.start()
        return copy

    early = [small(0, mask_hbm, mask_ref), small(1, base_hbm, base_ref)]
    for k in range(steps):
        a_copy(0, k).start()
        b_copy(k).start()
    for k in range(steps):
        a_copy(1, k).start()
    late = [small(2, order_hbm, order_v), small(3, inv_hbm, inv_ref), small(4, order_hbm, order_s)]

    barrier = pltpu.get_barrier_semaphore()

    def greet(axis, me, n):
        @pl.loop(1, n)
        def _(d):
            pl.semaphore_signal(barrier, inc=1, device_id={axis: lax.rem(me + d, n)}, device_id_type=MESH)

    greet("gz", g, ng)
    greet("row", r, nr)
    greet("col", c, nc)

    def landed(ref, sem):
        pltpu.make_async_remote_copy(
            src_ref=ref, dst_ref=ref, send_sem=sem, recv_sem=sem, device_id={"gz": g}, device_id_type=MESH
        ).wait_recv()

    def sent(ref, sem):
        pltpu.make_async_remote_copy(
            src_ref=ref, dst_ref=ref, send_sem=sem, recv_sem=sem, device_id={"gz": g}, device_id_type=MESH
        ).wait_send()

    def strips(n):
        return part.at[pl.ds(0, n * ch), :]

    def rs_copy(p, i):
        half = lax.rem(p + swap, 2)
        q = half * ng + i
        dest = jnp.where(first, i, q // 2)
        h = jnp.where(first, half, lax.rem(q, 2))
        return dest, pltpu.make_async_remote_copy(
            src_ref=part.at[pl.ds(pl.multiple_of(p * bs + i * ch, ch), ch), :],
            dst_ref=land.at[h, g],
            send_sem=rs_send,
            recv_sem=rs_recv.at[h],
            device_id={"gz": dest},
            device_id_type=MESH,
        )

    for p in range(2):
        top = p * bs
        half = lax.rem(p + swap, 2)
        at_once = (1, 2)[p]
        for k in range(0, steps, at_once):
            for n in range(k, k + at_once):
                if p == 0:
                    b_copy(n).wait()
                a_copy(p, n).wait()
            along = slice(k * depth, (k + at_once) * depth)
            for low in range(top, top + bs, bs // 2):
                term = dot(a_v[low : low + bs // 2, along], b_v[along, :])
                if k == 0:
                    part[low : low + bs // 2, :] = term
                else:
                    part[low : low + bs // 2, :] += term
        if p == 0:
            for copy in early:
                copy.wait()
        for i in range(bs // mb):
            for j in range(bs // mb):
                at = (slice(top + i * mb, top + (i + 1) * mb), slice(j * mb, (j + 1) * mb))
                part[at] = part[at] * mask_ref[0, j, half * (bs // mb) + i].astype(F32)

        @pl.when(g // (ng // 2) == half)
        def _():
            mine = pl.ds(pl.multiple_of(top + lax.rem(g, ng // 2) * rows, rows), rows)
            part[mine, :] = part[mine, :] + base_ref[...]

        if p == 0:
            pl.semaphore_wait(barrier, ng + nr + nc - 3)

        for d in far_first + [0]:
            i = lax.rem(d + g, ng)
            dest, copy = rs_copy(p, i)

            @pl.when(dest != g)
            def _():
                copy.start()

    def gather_copy(buf, n, j, d):
        return pltpu.make_async_remote_copy(
            src_ref=buf.at[j, g],
            dst_ref=buf.at[j, g],
            send_sem=ag_send.at[n, j],
            recv_sem=ag_recv.at[n, j],
            device_id={"gz": lax.rem(g + d, ng)},
            device_id_type=MESH,
        )

    def down_ref(m):
        return (f0.at[0, g], f0.at[1, g], raw.at[0], raw.at[1], x0.at[pl.ds(rows, ch), :])[m]

    def down_copy(m, d):
        return pltpu.make_async_remote_copy(
            src_ref=down_ref(m),
            dst_ref=down_ref(m),
            send_sem=z_send.at[m],
            recv_sem=z_recv.at[m],
            device_id={"row": d},
            device_id_type=MESH,
        )

    def down(m):
        @pl.when(first & (c == 0 if m == 4 else c > m // 2))
        def _():
            @pl.loop(1, nr)
            def _(d):
                down_copy(m, d).start()

    def down_end(m):
        @pl.when(first & (c == 0 if m == 4 else c > m // 2))
        def _():
            sent(strips(nr - 1) if m == 4 else f0.at[0, pl.ds(0, nr - 1)], z_send.at[m])

    def arrived(m):
        down_copy(m, 0).wait_recv()

    def gather(buf, n, j):
        @pl.when(first | (c > n))
        def _():
            for d in far_first:
                reads = others | (lax.rem(g + d, ng) >= n * (ng // 2))

                @pl.when(reads)
                def _():
                    gather_copy(buf, n, j, d).start()

    def gather_end(buf, n, j):
        def ended(count):
            sent(buf.at[j, pl.ds(0, count)], ag_send.at[n, j])

        if n == 0:
            pl.when(first | (c > n))(lambda: ended(ng - 1))
        else:
            pl.when(others & (c > n))(lambda: ended(ng - 1))
            pl.when(first & (g < ng // 2))(lambda: ended(ng // 2))
            if ng > 2:
                pl.when(first & (g >= ng // 2))(lambda: ended(ng // 2 - 1))

    def shared(buf, n, j):
        landed(buf.at[j, pl.ds(0, ng - 1)], ag_recv.at[n, j])

    def column_part(m, which=None):
        if m == 1:
            return x0.at[pl.ds(rows, ch), :]
        if m == 2:
            return x1.at[which]
        if which is None:
            return x0.at[pl.ds(0, rows), :]
        return x0.at[pl.ds(pl.multiple_of(which * ch, ch), ch), :]

    def column_copy(m, d, which=None):
        ref = column_part(m, which)
        return pltpu.make_async_remote_copy(
            src_ref=ref,
            dst_ref=ref,
            send_sem=x_send.at[m],
            recv_sem=x_recv.at[m],
            device_id={"col": d},
            device_id_type=MESH,
        )

    def sibling_copy(m, which):
        ref = column_part(m, which)
        return pltpu.make_async_remote_copy(
            src_ref=ref,
            dst_ref=ref,
            send_sem=s_send.at[m],
            recv_sem=s_recv.at[m],
            device_id={"col": c + 1 - 2 * core},
            device_id_type=MESH,
        )

    def columns(m, only=None):
        @pl.when(c == 0 if m == 1 else others & (c == m // 2))
        def _():
            @pl.loop(1 if m == 1 else 2, nc)
            def _(d):
                if m == 1:
                    pl.when(first | (d > 1))(lambda: column_copy(m, d).start())
                elif only is None:
                    column_copy(m, d, lax.rem(d, 2)).start()
                else:
                    pl.when(lax.rem(d, 2) == only)(lambda: column_copy(m, d, only).start())

    def columns_end(m):
        if m == 1:
            pl.when(first & (c == 0))(lambda: sent(strips(nc - 1), x_send.at[m]))
            pl.when(others & (c == 0))(lambda: sent(strips(nc - 2), x_send.at[m]))
        else:
            count = nc if m == 0 else nc - 2
            pl.when(others & (c == m // 2))(lambda: sent(strips(count), x_send.at[m]))

    def pass_on(m):
        column_copy(m, 1, core).wait_recv()
        sibling_copy(m, core).start()

    def passed_on(m):
        sibling_copy(m, 1 - core).wait_recv()

    for copy in late:
        copy.wait()

    for p in range(2):
        placer = (lax.broadcasted_iota(jnp.int32, (bs, bs), 0) == order_v[p : p + 1, :]).astype(BF16)
        for plain, ref in zip(split(inv_ref[p]), (m_hi, m_lo)):
            moved = lax.dot_general(plain, placer, (((1,), (1,)), ((), ())), preferred_element_type=F32)
            ref[p] = jnp.where(c == p, plain.astype(F32), moved).astype(BF16)

    for n in range(2):
        h = lax.rem(n + swap, 2)
        start = jnp.where(first, n * bs + g * ch, g * rows + n * ch)
        landed(land.at[h, pl.ds(0, ng - 1)], rs_recv.at[h])
        land[h, g] = part[pl.ds(pl.multiple_of(start, ch), ch), :]
        total = land[h, 0]
        for m in range(1, ng):
            total = total + land[h, m]
        own[pl.ds(pl.multiple_of(h * ch, ch), ch), :] = total

        def panel_0_rows():
            for j, cols in enumerate(halves):
                f0[j, g] = own[:ch, cols]

        def panel_1_rows():
            for j, cols in enumerate(halves):
                raw[j] = own[ch:, cols]

        if n == 0:

            @pl.when(first & (c == 0))
            def _():
                x0[rows:, :] = own[ch:, :]
                columns(1)

            pl.when(first & (c > 0))(panel_0_rows)
            for m in (4, 0, 1):
                down(m)

            @pl.when(first & (c > 0))
            def _():
                for j in range(2):
                    gather(f0, 0, j)
        else:
            pl.when(first & (c > 0))(panel_1_rows)
            pl.when(first & (c == 0))(panel_0_rows)
            down(2)
            down(3)

            @pl.when(first & (c == 0))
            def _():
                for j in range(2):
                    gather(f0, 0, j)

    @pl.when(others & (c == 0))
    def _():
        x0[:rows, :] = own[...]
        column_copy(0, 1).start()
        arrived(4)
        columns(1)
        columns(0)

    @pl.when(others & (c > 0))
    def _():
        for j in range(2):
            arrived(j)
            gather(f0, 0, j)

    @pl.when(first | (c > 1))
    def _():
        @pl.when(c > 0)
        def _():
            column_copy(1, 1).wait_recv()

        lower = dot3(split(x0[rows:, :]), m_hi[0], m_lo[0])
        parts = split(lower)

        for j, cols in enumerate(halves):

            @pl.when(others)
            def _():
                arrived(2 + j)

            shared(f0, 0, j)

            @pl.when(c == 0)
            def _():
                f1[j, g] = lower[:, cols]

            @pl.when(c > 0)
            def _():
                f1[j, g] = raw[j] - dot3(parts, *split(f0[j].reshape(bs, -1)))

            gather(f1, 1, j)

    @pl.when(others)
    def _():
        @pl.when(c == 1)
        def _():
            column_copy(0, 1).wait_recv()

        @pl.when(c > 1)
        def _():
            pass_on(0)
            passed_on(0)

        lower = dot3(split(x0[:rows, :]), m_hi[0], m_lo[0])
        parts = split(lower)

        @pl.when(c == 0)
        def _():
            own[...] = lower

        @pl.when(c > 0)
        def _():
            for j, cols in enumerate(halves):

                @pl.when(c == 1)
                def _():
                    shared(f0, 0, j)

                own[:, cols] = own[:, cols] - dot3(parts, *split(f0[j].reshape(bs, -1)))

                @pl.when(c == 1)
                def _():
                    x1[j] = own[:, cols]
                    columns(2, j)

    sent(strips(2 * (ng - 1)), rs_send)
    for m in range(5):
        down_end(m)
    for m in range(2):
        columns_end(m)
    for j in range(2):
        gather_end(f0, 0, j)
    pl.when(others & (c > 1))(lambda: sibling_copy(0, core).wait_send())

    @pl.when(others & (c == 1))
    def _():
        out_ref[...] = dot3(split(own[...]), m_hi[1], m_lo[1])

    @pl.when(others & (c == 0))
    def _():
        out_ref[...] = own[...]

    @pl.when(others & (c > 1))
    def _():
        pass_on(2)
        passed_on(2)
        lower = 0.0
        for j, cols in enumerate(halves):
            lower = lower + dot3(split(x1[j]), m_hi[1, cols, :], m_lo[1, cols, :])
        lower_parts = split(lower)
        for j, cols in enumerate(halves):
            shared(f1, 1, j)
            out_ref[:, cols] = own[:, cols] - dot3(lower_parts, *split(f1[j].reshape(bs, -1)))

    @pl.when(first)
    def _():
        def place(buf, p):
            @pl.loop(0, rows, unroll=8)
            def _(i):
                src = order_s[p, g % (ng // 2) * rows + i]
                row = [buf[j, src // ch, pl.ds(src % ch, 1), :] for j in range(2)]
                out_ref[pl.ds(i, 1), :] = jnp.concatenate(row, axis=1)

        @pl.when(g < ng // 2)
        def _():
            place(f0, 0)

        @pl.when(g >= ng // 2)
        def _():
            for j in range(2):
                shared(f1, 1, j)
            place(f1, 1)

    columns_end(2)
    for j in range(2):
        gather_end(f1, 1, j)
    pl.when(others & (c > 1))(lambda: sibling_copy(2, core).wait_send())


def on_device(ng, nr, nc, lower_sub, upper_sub, block_mask, front_base, pivot_inverse, pivot_order):
    slab, width = lower_sub.shape[1:]
    rows, cols = front_base.shape
    bs = pivot_inverse.shape[1]
    assert slab == 2 * bs and cols == bs and rows * ng == slab and pivot_inverse.shape[0] == 2
    ch = rows // 2
    steps = 4
    tiles = jnp.swapaxes(block_mask, 1, 2)
    operands = (lower_sub, upper_sub, tiles, front_base, pivot_inverse, pivot_order)
    vmem = pl.BlockSpec(memory_space=pltpu.VMEM)
    hbm = pl.BlockSpec(memory_space=pltpu.HBM)
    dma = pltpu.SemaphoreType.DMA
    return pl.pallas_call(
        functools.partial(kernel, ng, nr, nc, steps),
        out_shape=jax.ShapeDtypeStruct((rows, cols), F32),
        in_specs=[hbm] * 6,
        out_specs=vmem,
        scratch_shapes=[
            pltpu.VMEM((slab, width), BF16),
            pltpu.VMEM((width, cols), BF16),
            pltpu.SMEM(tiles.shape, jnp.int32),
            pltpu.VMEM((rows, cols), F32),
            pltpu.VMEM(pivot_inverse.shape, F32),
            pltpu.VMEM(pivot_order.shape, jnp.int32),
            pltpu.SMEM(pivot_order.shape, jnp.int32),
            pltpu.VMEM((slab, cols), F32),
            pltpu.VMEM((2, ng, ch, cols), F32),
            pltpu.VMEM((rows, cols), F32),
            pltpu.VMEM((2, ch, cols // 2), F32),
            pltpu.VMEM((2, ng, ch, cols // 2), F32),
            pltpu.VMEM((2, ng, ch, cols // 2), F32),
            pltpu.VMEM((rows + ch, bs), F32),
            pltpu.VMEM((2, rows, bs // 2), F32),
            pltpu.VMEM((2, bs, bs), BF16),
            pltpu.VMEM((2, bs, bs), BF16),
            dma((2, steps)),
            dma((steps,)),
            dma((5,)),
            dma(()),
            dma((2,)),
            dma((5,)),
            dma((5,)),
            dma((2, 2)),
            dma((2, 2)),
            dma((3,)),
            dma((3,)),
            dma((3,)),
            dma((3,)),
        ],
        compiler_params=pltpu.CompilerParams(
            collective_id=0, has_side_effects=True, vmem_limit_bytes=VMEM
        ),
    )(*[pltpu.with_memory_space_constraint(x, pltpu.HBM) for x in operands])


def solution(mesh):
    placed = (
        P("gz", "row", None),
        P("gz", None, "col"),
        P("gz", "row", "col"),
        P(("row", "gz"), "col"),
        P(),
        P(),
    )
    shape = mesh.shape
    return jax.shard_map(
        functools.partial(on_device, shape["gz"], shape["row"], shape["col"]),
        mesh=mesh,
        in_specs=placed,
        out_specs=P(("row", "gz"), "col"),
        check_vma=False,
    )
```

```python
import functools

import jax
import jax.numpy as jnp
from jax import lax
from jax.experimental import pallas as pl
from jax.experimental.pallas import tpu as pltpu
from jax.sharding import PartitionSpec as P

F32 = jnp.float32
BF16 = jnp.bfloat16
VMEM = 48 * 1024 * 1024
MESH = pl.DeviceIdType.MESH


def split(x):
    hi = x.astype(BF16)
    return hi, (x - hi.astype(F32)).astype(BF16)


def dot(a, b):
    return jnp.dot(a, b, preferred_element_type=F32)


def dot3(x, w_hi, w_lo):
    hi, lo = x
    n = hi.shape[0]
    both = dot(jnp.concatenate([hi, lo], axis=0), w_hi)
    return both[:n] + (both[n:] + dot(hi, w_lo))


def kernel(
    ng, nr, nc, steps,
    a_hbm, b_hbm, mask_hbm, base_hbm, inv_hbm, order_hbm,
    out_ref,
    a_v, b_v, mask_ref, base_ref, inv_ref, order_v, order_s,
    part, land, own, raw, f0, f1, x0, x1, m_hi, m_lo,
    a_sem, b_sem, in_sem, rs_send, rs_recv,
    z_send, z_recv, ag_send, ag_recv, x_send, x_recv, s_send, s_recv,
):
    g, r, c = lax.axis_index("gz"), lax.axis_index("row"), lax.axis_index("col")
    bs = inv_ref.shape[1]
    rows = own.shape[0]
    ch = rows // 2
    depth = a_v.shape[1] // steps
    mb = bs // mask_ref.shape[1]
    first = r == 0
    core = lax.rem(c, 2)
    far_first = sorted(range(1, ng), key=lambda d: abs(2 * d - ng))
    others = jnp.logical_not(first)
    swap = jnp.where(first & (c == 0), 1, 0)
    halves = [slice(j * bs // 2, (j + 1) * bs // 2) for j in range(2)]

    def a_copy(h, k):
        return pltpu.make_async_copy(
            a_hbm.at[0, pl.ds(pl.multiple_of(lax.rem(h + swap, 2) * bs, bs), bs), pl.ds(k * depth, depth)],
            a_v.at[pl.ds(h * bs, bs), pl.ds(k * depth, depth)],
            a_sem.at[h, k],
        )

    def b_copy(k):
        return pltpu.make_async_copy(b_hbm.at[0, pl.ds(k * depth, depth), :], b_v.at[pl.ds(k * depth, depth), :], b_sem.at[k])

    def small(n, src, dst):
        copy = pltpu.make_async_copy(src, dst, in_sem.at[n])
        copy.start()
        return copy

    barrier = pltpu.get_barrier_semaphore()

    def greet(axis, me, n):
        @pl.loop(1, n)
        def _(d):
            pl.semaphore_signal(barrier, inc=1, device_id={axis: lax.rem(me + d, n)}, device_id_type=MESH)

    greet("row", r, nr)
    greet("gz", g, ng)
    greet("col", c, nc)

    early = [small(0, mask_hbm, mask_ref), small(1, base_hbm, base_ref)]
    for k in range(steps):
        a_copy(0, k).start()
        b_copy(k).start()
    for k in range(steps):
        a_copy(1, k).start()
    late = [small(2, order_hbm, order_v), small(3, inv_hbm, inv_ref), small(4, order_hbm, order_s)]

    def landed(ref, sem):
        pltpu.make_async_remote_copy(
            src_ref=ref, dst_ref=ref, send_sem=sem, recv_sem=sem, device_id={"gz": g}, device_id_type=MESH
        ).wait_recv()

    def sent(ref, sem):
        pltpu.make_async_remote_copy(
            src_ref=ref, dst_ref=ref, send_sem=sem, recv_sem=sem, device_id={"gz": g}, device_id_type=MESH
        ).wait_send()

    def strips(n):
        return part.at[pl.ds(0, n * ch), :]

    def rs_copy(p, i):
        half = lax.rem(p + swap, 2)
        q = half * ng + i
        dest = jnp.where(first, i, q // 2)
        h = jnp.where(first, half, lax.rem(q, 2))
        return dest, pltpu.make_async_remote_copy(
            src_ref=part.at[pl.ds(pl.multiple_of(p * bs + i * ch, ch), ch), :],
            dst_ref=land.at[h, g],
            send_sem=rs_send,
            recv_sem=rs_recv.at[h],
            device_id={"gz": dest},
            device_id_type=MESH,
        )

    for p in range(2):
        top = p * bs
        half = lax.rem(p + swap, 2)
        at_once = (1, 2)[p]
        for k in range(0, steps, at_once):
            for n in range(k, k + at_once):
                if p == 0:
                    b_copy(n).wait()
                a_copy(p, n).wait()
            along = slice(k * depth, (k + at_once) * depth)
            for low in range(top, top + bs, bs // 2):
                term = dot(a_v[low : low + bs // 2, along], b_v[along, :])
                if k == 0:
                    part[low : low + bs // 2, :] = term
                else:
                    part[low : low + bs // 2, :] += term
        if p == 0:
            for copy in early:
                copy.wait()
        for i in range(bs // mb):
            for j in range(bs // mb):
                at = (slice(top + i * mb, top + (i + 1) * mb), slice(j * mb, (j + 1) * mb))
                part[at] = part[at] * mask_ref[0, j, half * (bs // mb) + i].astype(F32)

        @pl.when(g // (ng // 2) == half)
        def _():
            mine = pl.ds(pl.multiple_of(top + lax.rem(g, ng // 2) * rows, rows), rows)
            part[mine, :] = part[mine, :] + base_ref[...]

        if p == 0:
            pl.semaphore_wait(barrier, ng + nr + nc - 3)

        for d in far_first + [0]:
            i = lax.rem(d + g, ng)
            dest, copy = rs_copy(p, i)

            @pl.when(dest != g)
            def _():
                copy.start()

    def gather_copy(buf, n, j, d):
        return pltpu.make_async_remote_copy(
            src_ref=buf.at[j, g],
            dst_ref=buf.at[j, g],
            send_sem=ag_send.at[n, j],
            recv_sem=ag_recv.at[n, j],
            device_id={"gz": lax.rem(g + d, ng)},
            device_id_type=MESH,
        )

    def down_ref(m):
        return (f0.at[0, g], f0.at[1, g], raw.at[0], raw.at[1], x0.at[pl.ds(rows, ch), :])[m]

    def down_copy(m, d):
        return pltpu.make_async_remote_copy(
            src_ref=down_ref(m),
            dst_ref=down_ref(m),
            send_sem=z_send.at[m],
            recv_sem=z_recv.at[m],
            device_id={"row": d},
            device_id_type=MESH,
        )

    def down(m):
        @pl.when(first & (c == 0 if m == 4 else c > m // 2))
        def _():
            @pl.loop(1, nr)
            def _(d):
                down_copy(m, d).start()

    def down_end(m):
        @pl.when(first & (c == 0 if m == 4 else c > m // 2))
        def _():
            sent(strips(nr - 1) if m == 4 else f0.at[0, pl.ds(0, nr - 1)], z_send.at[m])

    def arrived(m):
        down_copy(m, 0).wait_recv()

    def gather(buf, n, j):
        @pl.when(first | (c > n))
        def _():
            for d in far_first:
                reads = others | (lax.rem(g + d, ng) >= n * (ng // 2))

                @pl.when(reads)
                def _():
                    gather_copy(buf, n, j, d).start()

    def gather_end(buf, n, j):
        def ended(count):
            sent(buf.at[j, pl.ds(0, count)], ag_send.at[n, j])

        if n == 0:
            pl.when(first | (c > n))(lambda: ended(ng - 1))
        else:
            pl.when(others & (c > n))(lambda: ended(ng - 1))
            pl.when(first & (g < ng // 2))(lambda: ended(ng // 2))
            if ng > 2:
                pl.when(first & (g >= ng // 2))(lambda: ended(ng // 2 - 1))

    def shared(buf, n, j):
        landed(buf.at[j, pl.ds(0, ng - 1)], ag_recv.at[n, j])

    def column_part(m, which=None):
        if m == 1:
            return x0.at[pl.ds(rows, ch), :]
        if m == 2:
            return x1.at[which]
        if which is None:
            return x0.at[pl.ds(0, rows), :]
        return x0.at[pl.ds(pl.multiple_of(which * ch, ch), ch), :]

    def column_copy(m, d, which=None):
        ref = column_part(m, which)
        return pltpu.make_async_remote_copy(
            src_ref=ref,
            dst_ref=ref,
            send_sem=x_send.at[m],
            recv_sem=x_recv.at[m],
            device_id={"col": d},
            device_id_type=MESH,
        )

    def sibling_copy(m, which):
        ref = column_part(m, which)
        return pltpu.make_async_remote_copy(
            src_ref=ref,
            dst_ref=ref,
            send_sem=s_send.at[m],
            recv_sem=s_recv.at[m],
            device_id={"col": c + 1 - 2 * core},
            device_id_type=MESH,
        )

    def columns(m, only=None):
        @pl.when(c == 0 if m == 1 else others & (c == m // 2))
        def _():
            @pl.loop(1 if m == 1 else 2, nc)
            def _(d):
                if m == 1:
                    pl.when(first | (d > 1))(lambda: column_copy(m, d).start())
                elif only is None:
                    column_copy(m, d, lax.rem(d, 2)).start()
                else:
                    pl.when(lax.rem(d, 2) == only)(lambda: column_copy(m, d, only).start())

    def columns_end(m):
        if m == 1:
            pl.when(first & (c == 0))(lambda: sent(strips(nc - 1), x_send.at[m]))
            pl.when(others & (c == 0))(lambda: sent(strips(nc - 2), x_send.at[m]))
        else:
            count = nc if m == 0 else nc - 2
            pl.when(others & (c == m // 2))(lambda: sent(strips(count), x_send.at[m]))

    def pass_on(m):
        column_copy(m, 1, core).wait_recv()
        sibling_copy(m, core).start()

    def passed_on(m):
        sibling_copy(m, 1 - core).wait_recv()

    for copy in late:
        copy.wait()

    for p in range(2):
        placer = (lax.broadcasted_iota(jnp.int32, (bs, bs), 0) == order_v[p : p + 1, :]).astype(BF16)
        for plain, ref in zip(split(inv_ref[p]), (m_hi, m_lo)):
            moved = lax.dot_general(plain, placer, (((1,), (1,)), ((), ())), preferred_element_type=F32)
            ref[p] = jnp.where(c == p, plain.astype(F32), moved).astype(BF16)

    for n in range(2):
        h = lax.rem(n + swap, 2)
        start = jnp.where(first, n * bs + g * ch, g * rows + n * ch)
        landed(land.at[h, pl.ds(0, ng - 1)], rs_recv.at[h])
        land[h, g] = part[pl.ds(pl.multiple_of(start, ch), ch), :]
        total = land[h, 0]
        for m in range(1, ng):
            total = total + land[h, m]
        own[pl.ds(pl.multiple_of(h * ch, ch), ch), :] = total

        def panel_0_rows():
            for j, cols in enumerate(halves):
                f0[j, g] = own[:ch, cols]

        def panel_1_rows():
            for j, cols in enumerate(halves):
                raw[j] = own[ch:, cols]

        if n == 0:

            @pl.when(first & (c == 0))
            def _():
                x0[rows:, :] = own[ch:, :]
                columns(1)

            pl.when(first & (c > 0))(panel_0_rows)
            for m in (4, 0, 1):
                down(m)

            @pl.when(first & (c > 0))
            def _():
                for j in range(2):
                    gather(f0, 0, j)
        else:
            pl.when(first & (c > 0))(panel_1_rows)
            pl.when(first & (c == 0))(panel_0_rows)
            down(2)
            down(3)

            @pl.when(first & (c == 0))
            def _():
                for j in range(2):
                    gather(f0, 0, j)

    @pl.when(others & (c == 0))
    def _():
        x0[:rows, :] = own[...]
        column_copy(0, 1).start()
        arrived(4)
        columns(1)
        columns(0)

    @pl.when(others & (c > 0))
    def _():
        for j in range(2):
            arrived(j)
            gather(f0, 0, j)

    @pl.when(first | (c > 1))
    def _():
        @pl.when(c > 0)
        def _():
            column_copy(1, 1).wait_recv()

        lower = dot3(split(x0[rows:, :]), m_hi[0], m_lo[0])
        parts = split(lower)

        for j, cols in enumerate(halves):

            @pl.when(others)
            def _():
                arrived(2 + j)

            shared(f0, 0, j)

            @pl.when(c == 0)
            def _():
                f1[j, g] = lower[:, cols]

            @pl.when(c > 0)
            def _():
                f1[j, g] = raw[j] - dot3(parts, *split(f0[j].reshape(bs, -1)))

            gather(f1, 1, j)

    @pl.when(others)
    def _():
        @pl.when(c == 1)
        def _():
            column_copy(0, 1).wait_recv()

        @pl.when(c > 1)
        def _():
            pass_on(0)
            passed_on(0)

        lower = dot3(split(x0[:rows, :]), m_hi[0], m_lo[0])
        parts = split(lower)

        @pl.when(c == 0)
        def _():
            own[...] = lower

        @pl.when(c > 0)
        def _():
            for j, cols in enumerate(halves):

                @pl.when(c == 1)
                def _():
                    shared(f0, 0, j)

                own[:, cols] = own[:, cols] - dot3(parts, *split(f0[j].reshape(bs, -1)))

                @pl.when(c == 1)
                def _():
                    x1[j] = own[:, cols]
                    columns(2, j)

    sent(strips(2 * (ng - 1)), rs_send)
    for m in range(5):
        down_end(m)
    for m in range(2):
        columns_end(m)
    for j in range(2):
        gather_end(f0, 0, j)
    pl.when(others & (c > 1))(lambda: sibling_copy(0, core).wait_send())

    @pl.when(others & (c == 1))
    def _():
        out_ref[...] = dot3(split(own[...]), m_hi[1], m_lo[1])

    @pl.when(others & (c == 0))
    def _():
        out_ref[...] = own[...]

    @pl.when(others & (c > 1))
    def _():
        pass_on(2)
        passed_on(2)
        lower = 0.0
        for j, cols in enumerate(halves):
            lower = lower + dot3(split(x1[j]), m_hi[1, cols, :], m_lo[1, cols, :])
        lower_parts = split(lower)
        for j, cols in enumerate(halves):
            shared(f1, 1, j)
            out_ref[:, cols] = own[:, cols] - dot3(lower_parts, *split(f1[j].reshape(bs, -1)))

    @pl.when(first)
    def _():
        def place(buf, p):
            @pl.loop(0, rows, unroll=8)
            def _(i):
                src = order_s[p, g % (ng // 2) * rows + i]
                row = [buf[j, src // ch, pl.ds(src % ch, 1), :] for j in range(2)]
                out_ref[pl.ds(i, 1), :] = jnp.concatenate(row, axis=1)

        @pl.when(g < ng // 2)
        def _():
            place(f0, 0)

        @pl.when(g >= ng // 2)
        def _():
            for j in range(2):
                shared(f1, 1, j)
            place(f1, 1)

    columns_end(2)
    for j in range(2):
        gather_end(f1, 1, j)
    pl.when(others & (c > 1))(lambda: sibling_copy(2, core).wait_send())


def on_device(ng, nr, nc, lower_sub, upper_sub, block_mask, front_base, pivot_inverse, pivot_order):
    slab, width = lower_sub.shape[1:]
    rows, cols = front_base.shape
    bs = pivot_inverse.shape[1]
    assert slab == 2 * bs and cols == bs and rows * ng == slab and pivot_inverse.shape[0] == 2
    ch = rows // 2
    steps = 4
    tiles = jnp.swapaxes(block_mask, 1, 2)
    operands = (lower_sub, upper_sub, tiles, front_base, pivot_inverse, pivot_order)
    vmem = pl.BlockSpec(memory_space=pltpu.VMEM)
    hbm = pl.BlockSpec(memory_space=pltpu.HBM)
    dma = pltpu.SemaphoreType.DMA
    return pl.pallas_call(
        functools.partial(kernel, ng, nr, nc, steps),
        out_shape=jax.ShapeDtypeStruct((rows, cols), F32),
        in_specs=[hbm] * 6,
        out_specs=vmem,
        scratch_shapes=[
            pltpu.VMEM((slab, width), BF16),
            pltpu.VMEM((width, cols), BF16),
            pltpu.SMEM(tiles.shape, jnp.int32),
            pltpu.VMEM((rows, cols), F32),
            pltpu.VMEM(pivot_inverse.shape, F32),
            pltpu.VMEM(pivot_order.shape, jnp.int32),
            pltpu.SMEM(pivot_order.shape, jnp.int32),
            pltpu.VMEM((slab, cols), F32),
            pltpu.VMEM((2, ng, ch, cols), F32),
            pltpu.VMEM((rows, cols), F32),
            pltpu.VMEM((2, ch, cols // 2), F32),
            pltpu.VMEM((2, ng, ch, cols // 2), F32),
            pltpu.VMEM((2, ng, ch, cols // 2), F32),
            pltpu.VMEM((rows + ch, bs), F32),
            pltpu.VMEM((2, rows, bs // 2), F32),
            pltpu.VMEM((2, bs, bs), BF16),
            pltpu.VMEM((2, bs, bs), BF16),
            dma((2, steps)),
            dma((steps,)),
            dma((5,)),
            dma(()),
            dma((2,)),
            dma((5,)),
            dma((5,)),
            dma((2, 2)),
            dma((2, 2)),
            dma((3,)),
            dma((3,)),
            dma((3,)),
            dma((3,)),
        ],
        compiler_params=pltpu.CompilerParams(
            collective_id=0, has_side_effects=True, vmem_limit_bytes=VMEM
        ),
    )(*[pltpu.with_memory_space_constraint(x, pltpu.HBM) for x in operands])


def solution(mesh):
    placed = (
        P("gz", "row", None),
        P("gz", None, "col"),
        P("gz", "row", "col"),
        P(("row", "gz"), "col"),
        P(),
        P(),
    )
    shape = mesh.shape
    return jax.shard_map(
        functools.partial(on_device, shape["gz"], shape["row"], shape["col"]),
        mesh=mesh,
        in_specs=placed,
        out_specs=P(("row", "gz"), "col"),
        check_vma=False,
    )
```

```python
import functools

import jax
import jax.numpy as jnp
from jax import lax
from jax.experimental import pallas as pl
from jax.experimental.pallas import tpu as pltpu
from jax.sharding import PartitionSpec as P

F32 = jnp.float32
BF16 = jnp.bfloat16
VMEM = 48 * 1024 * 1024
MESH = pl.DeviceIdType.MESH


def split(x):
    hi = x.astype(BF16)
    return hi, (x - hi.astype(F32)).astype(BF16)


def dot(a, b):
    return jnp.dot(a, b, preferred_element_type=F32)


def dot3(x, w_hi, w_lo):
    hi, lo = x
    n = hi.shape[0]
    both = dot(jnp.concatenate([hi, lo], axis=0), w_hi)
    return both[:n] + (both[n:] + dot(hi, w_lo))


def kernel(
    ng, nr, nc, steps,
    a_hbm, b_hbm, mask_hbm, base_hbm, inv_hbm, order_hbm,
    out_ref,
    a_v, b_v, mask_ref, base_ref, inv_ref, order_v, order_s,
    part, land, own, raw, f0, f1, x0, x1, m_hi, m_lo,
    a_sem, b_sem, in_sem, rs_send, rs_recv,
    z_send, z_recv, ag_send, ag_recv, x_send, x_recv, s_send, s_recv,
):
    g, r, c = lax.axis_index("gz"), lax.axis_index("row"), lax.axis_index("col")
    bs = inv_ref.shape[1]
    rows = own.shape[0]
    ch = rows // 2
    depth = a_v.shape[1] // steps
    mb = bs // mask_ref.shape[1]
    first = r == 0
    core = lax.rem(c, 2)
    far_chips = sorted(range(2, nc), key=lambda d: -min(d // 2, (nc - d + 1) // 2))
    far_first = sorted(range(1, ng), key=lambda d: abs(2 * d - ng))
    others = jnp.logical_not(first)
    swap = jnp.where(first & (c == 0), 1, 0)
    halves = [slice(j * bs // 2, (j + 1) * bs // 2) for j in range(2)]

    def a_copy(h, k):
        return pltpu.make_async_copy(
            a_hbm.at[0, pl.ds(pl.multiple_of(lax.rem(h + swap, 2) * bs, bs), bs), pl.ds(k * depth, depth)],
            a_v.at[pl.ds(h * bs, bs), pl.ds(k * depth, depth)],
            a_sem.at[h, k],
        )

    def b_copy(k):
        return pltpu.make_async_copy(b_hbm.at[0, pl.ds(k * depth, depth), :], b_v.at[pl.ds(k * depth, depth), :], b_sem.at[k])

    def small(n, src, dst):
        copy = pltpu.make_async_copy(src, dst, in_sem.at[n])
        copy.start()
        return copy

    barrier = pltpu.get_barrier_semaphore()

    def greet(axis, me, n):
        @pl.loop(1, n)
        def _(d):
            pl.semaphore_signal(barrier, inc=1, device_id={axis: lax.rem(me + d, n)}, device_id_type=MESH)

    greet("row", r, nr)
    greet("gz", g, ng)
    greet("col", c, nc)

    early = [small(0, mask_hbm, mask_ref), small(1, base_hbm, base_ref)]
    for k in range(steps):
        a_copy(0, k).start()
        b_copy(k).start()
    for k in range(steps):
        a_copy(1, k).start()
    late = [small(2, order_hbm, order_v), small(3, inv_hbm, inv_ref), small(4, order_hbm, order_s)]

    def landed(ref, sem):
        pltpu.make_async_remote_copy(
            src_ref=ref, dst_ref=ref, send_sem=sem, recv_sem=sem, device_id={"gz": g}, device_id_type=MESH
        ).wait_recv()

    def sent(ref, sem):
        pltpu.make_async_remote_copy(
            src_ref=ref, dst_ref=ref, send_sem=sem, recv_sem=sem, device_id={"gz": g}, device_id_type=MESH
        ).wait_send()

    def strips(n):
        return part.at[pl.ds(0, n * ch), :]

    def rs_copy(p, i):
        half = lax.rem(p + swap, 2)
        q = half * ng + i
        dest = jnp.where(first, i, q // 2)
        h = jnp.where(first, half, lax.rem(q, 2))
        return dest, pltpu.make_async_remote_copy(
            src_ref=part.at[pl.ds(pl.multiple_of(p * bs + i * ch, ch), ch), :],
            dst_ref=land.at[h, g],
            send_sem=rs_send,
            recv_sem=rs_recv.at[h],
            device_id={"gz": dest},
            device_id_type=MESH,
        )

    for p in range(2):
        top = p * bs
        half = lax.rem(p + swap, 2)
        at_once = (1, 2)[p]
        for k in range(0, steps, at_once):
            for n in range(k, k + at_once):
                if p == 0:
                    b_copy(n).wait()
                a_copy(p, n).wait()
            along = slice(k * depth, (k + at_once) * depth)
            for low in range(top, top + bs, bs // 2):
                term = dot(a_v[low : low + bs // 2, along], b_v[along, :])
                if k == 0:
                    part[low : low + bs // 2, :] = term
                else:
                    part[low : low + bs // 2, :] += term
        if p == 0:
            for copy in early:
                copy.wait()
        for i in range(bs // mb):
            for j in range(bs // mb):
                at = (slice(top + i * mb, top + (i + 1) * mb), slice(j * mb, (j + 1) * mb))
                part[at] = part[at] * mask_ref[0, j, half * (bs // mb) + i].astype(F32)

        @pl.when(g // (ng // 2) == half)
        def _():
            mine = pl.ds(pl.multiple_of(top + lax.rem(g, ng // 2) * rows, rows), rows)
            part[mine, :] = part[mine, :] + base_ref[...]

        if p == 0:
            pl.semaphore_wait(barrier, ng + nr + nc - 3)

        for d in far_first + [0]:
            i = lax.rem(d + g, ng)
            dest, copy = rs_copy(p, i)

            @pl.when(dest != g)
            def _():
                copy.start()

    def gather_copy(buf, n, j, d):
        return pltpu.make_async_remote_copy(
            src_ref=buf.at[j, g],
            dst_ref=buf.at[j, g],
            send_sem=ag_send.at[n, j],
            recv_sem=ag_recv.at[n, j],
            device_id={"gz": lax.rem(g + d, ng)},
            device_id_type=MESH,
        )

    def down_ref(m):
        return (f0.at[0, g], f0.at[1, g], raw.at[0], raw.at[1], x0.at[pl.ds(rows, ch), :])[m]

    def down_copy(m, d):
        return pltpu.make_async_remote_copy(
            src_ref=down_ref(m),
            dst_ref=down_ref(m),
            send_sem=z_send.at[m],
            recv_sem=z_recv.at[m],
            device_id={"row": d},
            device_id_type=MESH,
        )

    def down(m):
        @pl.when(first & (c == 0 if m == 4 else c > m // 2))
        def _():
            @pl.loop(1, nr)
            def _(d):
                down_copy(m, d).start()

    def down_end(m):
        @pl.when(first & (c == 0 if m == 4 else c > m // 2))
        def _():
            sent(strips(nr - 1) if m == 4 else f0.at[0, pl.ds(0, nr - 1)], z_send.at[m])

    def arrived(m):
        down_copy(m, 0).wait_recv()

    def gather(buf, n, j):
        @pl.when(first | (c > n))
        def _():
            for d in far_first:
                reads = others | (lax.rem(g + d, ng) >= n * (ng // 2))

                @pl.when(reads)
                def _():
                    gather_copy(buf, n, j, d).start()

    def gather_end(buf, n, j):
        def ended(count):
            sent(buf.at[j, pl.ds(0, count)], ag_send.at[n, j])

        if n == 0:
            pl.when(first | (c > n))(lambda: ended(ng - 1))
        else:
            pl.when(others & (c > n))(lambda: ended(ng - 1))
            pl.when(first & (g < ng // 2))(lambda: ended(ng // 2))
            if ng > 2:
                pl.when(first & (g >= ng // 2))(lambda: ended(ng // 2 - 1))

    def shared(buf, n, j):
        landed(buf.at[j, pl.ds(0, ng - 1)], ag_recv.at[n, j])

    def column_part(m, which=None):
        if m == 1:
            return x0.at[pl.ds(rows, ch), :]
        if m == 2:
            return x1.at[which]
        if which is None:
            return x0.at[pl.ds(0, rows), :]
        return x0.at[pl.ds(pl.multiple_of(which * ch, ch), ch), :]

    def column_copy(m, d, which=None):
        ref = column_part(m, which)
        return pltpu.make_async_remote_copy(
            src_ref=ref,
            dst_ref=ref,
            send_sem=x_send.at[m],
            recv_sem=x_recv.at[m],
            device_id={"col": d},
            device_id_type=MESH,
        )

    def sibling_copy(m, which):
        ref = column_part(m, which)
        return pltpu.make_async_remote_copy(
            src_ref=ref,
            dst_ref=ref,
            send_sem=s_send.at[m],
            recv_sem=s_recv.at[m],
            device_id={"col": c + 1 - 2 * core},
            device_id_type=MESH,
        )

    def columns(m, only=None):
        @pl.when(c == 0 if m == 1 else others & (c == m // 2))
        def _():
            for d in ([1] if m == 1 else []) + far_chips:
                if m == 1:
                    pl.when(first | (d > 1))(lambda d=d: column_copy(m, d).start())
                elif only is None:
                    column_copy(m, d, d % 2).start()
                elif d % 2 == only:
                    column_copy(m, d, only).start()

    def columns_end(m):
        if m == 1:
            pl.when(first & (c == 0))(lambda: sent(strips(nc - 1), x_send.at[m]))
            pl.when(others & (c == 0))(lambda: sent(strips(nc - 2), x_send.at[m]))
        else:
            count = nc if m == 0 else nc - 2
            pl.when(others & (c == m // 2))(lambda: sent(strips(count), x_send.at[m]))

    def pass_on(m):
        column_copy(m, 1, core).wait_recv()
        sibling_copy(m, core).start()

    def passed_on(m):
        sibling_copy(m, 1 - core).wait_recv()

    for copy in late:
        copy.wait()

    for p in range(2):
        placer = (lax.broadcasted_iota(jnp.int32, (bs, bs), 0) == order_v[p : p + 1, :]).astype(BF16)
        for plain, ref in zip(split(inv_ref[p]), (m_hi, m_lo)):
            moved = lax.dot_general(plain, placer, (((1,), (1,)), ((), ())), preferred_element_type=F32)
            ref[p] = jnp.where(c == p, plain.astype(F32), moved).astype(BF16)

    for n in range(2):
        h = lax.rem(n + swap, 2)
        start = jnp.where(first, n * bs + g * ch, g * rows + n * ch)
        landed(land.at[h, pl.ds(0, ng - 1)], rs_recv.at[h])
        land[h, g] = part[pl.ds(pl.multiple_of(start, ch), ch), :]
        total = land[h, 0]
        for m in range(1, ng):
            total = total + land[h, m]
        own[pl.ds(pl.multiple_of(h * ch, ch), ch), :] = total

        def panel_0_rows():
            for j, cols in enumerate(halves):
                f0[j, g] = own[:ch, cols]

        def panel_1_rows():
            for j, cols in enumerate(halves):
                raw[j] = own[ch:, cols]

        if n == 0:

            @pl.when(first & (c == 0))
            def _():
                x0[rows:, :] = own[ch:, :]
                columns(1)

            pl.when(first & (c > 0))(panel_0_rows)
            for m in (4, 0, 1):
                down(m)

            @pl.when(first & (c > 0))
            def _():
                for j in range(2):
                    gather(f0, 0, j)
        else:
            pl.when(first & (c > 0))(panel_1_rows)
            pl.when(first & (c == 0))(panel_0_rows)
            down(2)
            down(3)

            @pl.when(first & (c == 0))
            def _():
                for j in range(2):
                    gather(f0, 0, j)

    @pl.when(others & (c == 0))
    def _():
        x0[:rows, :] = own[...]
        column_copy(0, 1).start()
        arrived(4)
        columns(1)
        columns(0)

    @pl.when(others & (c > 0))
    def _():
        for j in range(2):
            arrived(j)
            gather(f0, 0, j)

    @pl.when(first | (c > 1))
    def _():
        @pl.when(c > 0)
        def _():
            column_copy(1, 1).wait_recv()

        lower = dot3(split(x0[rows:, :]), m_hi[0], m_lo[0])
        parts = split(lower)

        for j, cols in enumerate(halves):

            @pl.when(others)
            def _():
                arrived(2 + j)

            shared(f0, 0, j)

            @pl.when(c == 0)
            def _():
                f1[j, g] = lower[:, cols]

            @pl.when(c > 0)
            def _():
                f1[j, g] = raw[j] - dot3(parts, *split(f0[j].reshape(bs, -1)))

            gather(f1, 1, j)

    @pl.when(others)
    def _():
        @pl.when(c == 1)
        def _():
            column_copy(0, 1).wait_recv()

        @pl.when(c > 1)
        def _():
            pass_on(0)
            passed_on(0)

        lower = dot3(split(x0[:rows, :]), m_hi[0], m_lo[0])
        parts = split(lower)

        @pl.when(c == 0)
        def _():
            own[...] = lower

        @pl.when(c > 0)
        def _():
            for j, cols in enumerate(halves):

                @pl.when(c == 1)
                def _():
                    shared(f0, 0, j)

                own[:, cols] = own[:, cols] - dot3(parts, *split(f0[j].reshape(bs, -1)))

                @pl.when(c == 1)
                def _():
                    x1[j] = own[:, cols]
                    columns(2, j)

    sent(strips(2 * (ng - 1)), rs_send)
    for m in range(5):
        down_end(m)
    for m in range(2):
        columns_end(m)
    for j in range(2):
        gather_end(f0, 0, j)
    pl.when(others & (c > 1))(lambda: sibling_copy(0, core).wait_send())

    @pl.when(others & (c == 1))
    def _():
        out_ref[...] = dot3(split(own[...]), m_hi[1], m_lo[1])

    @pl.when(others & (c == 0))
    def _():
        out_ref[...] = own[...]

    @pl.when(others & (c > 1))
    def _():
        pass_on(2)
        passed_on(2)
        lower = 0.0
        for j, cols in enumerate(halves):
            lower = lower + dot3(split(x1[j]), m_hi[1, cols, :], m_lo[1, cols, :])
        lower_parts = split(lower)
        for j, cols in enumerate(halves):
            shared(f1, 1, j)
            out_ref[:, cols] = own[:, cols] - dot3(lower_parts, *split(f1[j].reshape(bs, -1)))

    @pl.when(first)
    def _():
        def place(buf, p):
            @pl.loop(0, rows, unroll=8)
            def _(i):
                src = order_s[p, g % (ng // 2) * rows + i]
                row = [buf[j, src // ch, pl.ds(src % ch, 1), :] for j in range(2)]
                out_ref[pl.ds(i, 1), :] = jnp.concatenate(row, axis=1)

        @pl.when(g < ng // 2)
        def _():
            place(f0, 0)

        @pl.when(g >= ng // 2)
        def _():
            for j in range(2):
                shared(f1, 1, j)
            place(f1, 1)

    columns_end(2)
    for j in range(2):
        gather_end(f1, 1, j)
    pl.when(others & (c > 1))(lambda: sibling_copy(2, core).wait_send())


def on_device(ng, nr, nc, lower_sub, upper_sub, block_mask, front_base, pivot_inverse, pivot_order):
    slab, width = lower_sub.shape[1:]
    rows, cols = front_base.shape
    bs = pivot_inverse.shape[1]
    assert slab == 2 * bs and cols == bs and rows * ng == slab and pivot_inverse.shape[0] == 2
    ch = rows // 2
    steps = 4
    tiles = jnp.swapaxes(block_mask, 1, 2)
    operands = (lower_sub, upper_sub, tiles, front_base, pivot_inverse, pivot_order)
    vmem = pl.BlockSpec(memory_space=pltpu.VMEM)
    hbm = pl.BlockSpec(memory_space=pltpu.HBM)
    dma = pltpu.SemaphoreType.DMA
    return pl.pallas_call(
        functools.partial(kernel, ng, nr, nc, steps),
        out_shape=jax.ShapeDtypeStruct((rows, cols), F32),
        in_specs=[hbm] * 6,
        out_specs=vmem,
        scratch_shapes=[
            pltpu.VMEM((slab, width), BF16),
            pltpu.VMEM((width, cols), BF16),
            pltpu.SMEM(tiles.shape, jnp.int32),
            pltpu.VMEM((rows, cols), F32),
            pltpu.VMEM(pivot_inverse.shape, F32),
            pltpu.VMEM(pivot_order.shape, jnp.int32),
            pltpu.SMEM(pivot_order.shape, jnp.int32),
            pltpu.VMEM((slab, cols), F32),
            pltpu.VMEM((2, ng, ch, cols), F32),
            pltpu.VMEM((rows, cols), F32),
            pltpu.VMEM((2, ch, cols // 2), F32),
            pltpu.VMEM((2, ng, ch, cols // 2), F32),
            pltpu.VMEM((2, ng, ch, cols // 2), F32),
            pltpu.VMEM((rows + ch, bs), F32),
            pltpu.VMEM((2, rows, bs // 2), F32),
            pltpu.VMEM((2, bs, bs), BF16),
            pltpu.VMEM((2, bs, bs), BF16),
            dma((2, steps)),
            dma((steps,)),
            dma((5,)),
            dma(()),
            dma((2,)),
            dma((5,)),
            dma((5,)),
            dma((2, 2)),
            dma((2, 2)),
            dma((3,)),
            dma((3,)),
            dma((3,)),
            dma((3,)),
        ],
        compiler_params=pltpu.CompilerParams(
            collective_id=0, has_side_effects=True, vmem_limit_bytes=VMEM
        ),
    )(*[pltpu.with_memory_space_constraint(x, pltpu.HBM) for x in operands])


def solution(mesh):
    placed = (
        P("gz", "row", None),
        P("gz", None, "col"),
        P("gz", "row", "col"),
        P(("row", "gz"), "col"),
        P(),
        P(),
    )
    shape = mesh.shape
    return jax.shard_map(
        functools.partial(on_device, shape["gz"], shape["row"], shape["col"]),
        mesh=mesh,
        in_specs=placed,
        out_specs=P(("row", "gz"), "col"),
        check_vma=False,
    )
```
